32 devices in a mesh: dp: 2 (over core), fsdp: 16 (over z, y, x).
Axes of the slice: x: 2, y: 2, z: 4, core: 2. Of those that a mesh axis runs over, the one named last changes fastest.
Arguments:
- inputs: bfloat16 [32768, 768], P(('dp', 'fsdp')), may hold values from -6 to 6
- cotangent: bfloat16 [32768, 768], P(('dp', 'fsdp')), may hold values from -6 to 6
- lengths: int32 [64], P(('dp', 'fsdp')), may hold values from 128 to 512, as said below
- owner_slot: int32 [108], replicated, may hold values from 0 to 111, as said below
- weights: float32 [112, 256, 256], P('fsdp')
- vectors: float32 [9216], P('fsdp')
- left_stat: float32 [112, 256, 256], P('fsdp'), as said below
- right_stat: float32 [112, 256, 256], P('fsdp'), as said below
- left_root: float32 [112, 256, 256], P('fsdp'), as said below
- right_root: float32 [112, 256, 256], P('fsdp'), as said below
- vector_stat: float32 [9216], P('fsdp'), as said below
Outputs:
- outputs: bfloat16 [32768, 768], P(('dp', 'fsdp'))
- input_grad: bfloat16 [32768, 768], P(('dp', 'fsdp'))
- block_grads: float32 [112, 256, 256], P('fsdp')
- new_left: float32 [112, 256, 256], P('fsdp')
- new_right: float32 [112, 256, 256], P('fsdp')
- new_weights: float32 [112, 256, 256], P('fsdp')
- vector_grads: float32 [9216], P('fsdp')
- new_vector_stat: float32 [9216], P('fsdp')
- new_vectors: float32 [9216], P('fsdp')
The draws below stay inside these ranges and needn't reach their ends.
Inputs may be any that keep to these rules, and one draw needn't show every extreme that they name: `lengths`: each sentence has 128, 256 or 512 tokens. `owner_slot`: distinct slots, one for each block. `left_stat`: symmetric. `right_stat`: symmetric. `left_root`: symmetric. `right_root`: symmetric. `vector_stat`: positive.
All inputs are finite; a program needn't handle non-finite values.
Results may differ from the reference program's by a relative error of at most 0.017.
The reference program's roundings to bfloat16 on the way count: a program that leaves them out, or rounds other values in their place, can miss the bound.
Values may be sent and summed in bfloat16 or wider, within the bound.
A program may use at most 256 MiB of HBM per device.

```python
import math
import jax
import jax.numpy as jnp
from jax import lax

D = 768
HEADS = 12
HEAD = 64
FF = 3072
BLK = 256
MAXLEN = 512
SEQS = 64
TOKENS = 32768
NBLK = 108
SLOTS_ALL = 112
VEC = 9216


def owner_map(key):
    key = jax.random.fold_in(key, 11)
    inner = jax.random.permutation(key, SLOTS_ALL - 2)[:NBLK - 2].astype(jnp.int32) + 1
    ends = jnp.array([0, SLOTS_ALL - 1], jnp.int32)
    chosen = jnp.concatenate([ends, inner])
    order = jax.random.permutation(jax.random.fold_in(key, 12), NBLK)
    return chosen[order]


def grad_size():
    return 0.5 * math.sqrt(SEQS * MAXLEN * 7.0 / 12.0)


def log_uniform(key, shape, lower, upper):
    return jnp.exp(jax.random.uniform(key, shape, jnp.float32, math.log(lower), math.log(upper)))


def symmetric_normal(key, scale):
    base = jax.random.normal(key, (SLOTS_ALL, BLK, BLK), jnp.float32)
    return (base + jnp.swapaxes(base, 1, 2)) * (scale / math.sqrt(2.0))


def statistic(key):
    level = BLK * grad_size() ** 2
    diagonal = log_uniform(jax.random.fold_in(key, 1), (SLOTS_ALL, BLK), 1.0, 4.0) * level
    offdiag = symmetric_normal(jax.random.fold_in(key, 2), 0.5 * level / math.sqrt(BLK))
    eye = jnp.eye(BLK, dtype=jnp.float32)
    return offdiag * (1.0 - eye) + diagonal[:, :, None] * eye


def inverse_root(key):
    level = (BLK * grad_size() ** 2) ** (-0.25)
    diagonal = log_uniform(jax.random.fold_in(key, 1), (SLOTS_ALL, BLK), 0.5, 2.0)
    offdiag = symmetric_normal(jax.random.fold_in(key, 2), 0.5 / math.sqrt(BLK))
    eye = jnp.eye(BLK, dtype=jnp.float32)
    return (offdiag * (1.0 - eye) + diagonal[:, :, None] * eye) * level


def draw_owner_slot(key, part):
    return owner_map(key)


def draw_weights(key, part):
    slots = owner_map(key)
    key = jax.random.fold_in(key, 21)
    rows_d = D // BLK
    rows_f = FF // BLK
    scales = jnp.concatenate([jnp.full((3 * rows_d * rows_d,), 1.3 / math.sqrt(D), jnp.float32), jnp.full((rows_d * rows_d,), 4.0 / math.sqrt(D), jnp.float32), jnp.full((rows_d * rows_f,), 1.0 / math.sqrt(D), jnp.float32), jnp.full((rows_f * rows_d,), 1.5 / math.sqrt(FF), jnp.float32)])
    slot_scale = jnp.full((SLOTS_ALL,), 1.0 / math.sqrt(D), jnp.float32).at[slots].set(scales)
    values = jax.random.truncated_normal(key, -6.0, 6.0, (SLOTS_ALL, BLK, BLK), jnp.float32)
    return values * slot_scale[:, None, None]


def draw_vectors(key, part):
    key = jax.random.fold_in(key, 51)
    index = jnp.arange(VEC)
    is_gain = (index >= 3 * D) & (index < 4 * D) | (index >= 6 * D + FF) & (index < 7 * D + FF)
    gains = jax.random.uniform(jax.random.fold_in(key, 1), (VEC,), jnp.float32, 0.6, 1.4)
    biases = jax.random.truncated_normal(jax.random.fold_in(key, 2), -6.0, 6.0, (VEC,), jnp.float32) * 0.3
    return jnp.where(is_gain, gains, biases)


def draw_left_stat(key, part):
    key = jax.random.fold_in(key, 31)
    return statistic(key)


def draw_right_stat(key, part):
    key = jax.random.fold_in(key, 32)
    return statistic(key)


def draw_left_root(key, part):
    key = jax.random.fold_in(key, 41)
    return inverse_root(key)


def draw_right_root(key, part):
    key = jax.random.fold_in(key, 42)
    return inverse_root(key)


def draw_vector_stat(key, part):
    key = jax.random.fold_in(key, 61)
    return log_uniform(key, (VEC,), 1.0, 4.0) * grad_size() ** 2


def draw_lengths(key, part):
    key = jax.random.fold_in(key, 71)
    picks = jax.random.randint(key, (SEQS,), 0, 3)
    table = jnp.array([MAXLEN // 4, MAXLEN // 2, MAXLEN], jnp.int32)
    values = table[picks]
    return values.at[0].set(MAXLEN).at[1].set(MAXLEN // 4)


def levels(rng, shape, split, low, top_value):
    loudness = 1.0
    for dim, parts in split:
        draws = jax.random.uniform(jax.random.fold_in(jax.random.fold_in(rng, 6), dim), (parts,), jnp.float32, low / len(split), top_value / len(split))
        loudness = loudness * jnp.repeat(jnp.exp(draws), shape[dim] // parts).reshape((-1,) + (1,) * (len(shape) - 1 - dim))
    return loudness


def centred(rng, shape, deviation, bound, cuts=(), held_as=jnp.bfloat16):
    values = jax.random.normal(rng, shape, jnp.float32) * deviation
    if len(cuts) > 0:
        values = levels(rng, shape, cuts, -0.22, 0.18) * values
    return jnp.clip(values, min=-bound, max=bound).astype(held_as)


def setup_inputs(seed: int = 0) -> dict:
    splits = jax.random.split(jax.random.key(seed), 12)
    inputs = centred(splits[0], (TOKENS, D), 1.0, 6.0, ((0, 32),))
    cotangent = centred(splits[1], (TOKENS, D), 1.0, 6.0, ((0, 32),))
    lengths = draw_lengths(jax.random.fold_in(splits[11], 71), 0)
    owner_slot = draw_owner_slot(jax.random.fold_in(splits[11], 71), 0)
    weights = draw_weights(jax.random.fold_in(splits[11], 71), 0)
    vectors = draw_vectors(jax.random.fold_in(splits[11], 71), 0)
    left_stat = draw_left_stat(jax.random.fold_in(splits[11], 71), 0)
    right_stat = draw_right_stat(jax.random.fold_in(splits[11], 71), 0)
    left_root = draw_left_root(jax.random.fold_in(splits[11], 71), 0)
    right_root = draw_right_root(jax.random.fold_in(splits[11], 71), 0)
    vector_stat = draw_vector_stat(jax.random.fold_in(splits[11], 71), 0)
    return dict(inputs=inputs, cotangent=cotangent, lengths=lengths, owner_slot=owner_slot, weights=weights, vectors=vectors, left_stat=left_stat, right_stat=right_stat, left_root=left_root, right_root=right_root, vector_stat=vector_stat)


@jax.custom_vjp
def low(v):
    return lax.optimization_barrier(v.astype(jnp.bfloat16)).astype(jnp.float32)

@jax.custom_vjp
def low_back(v):
    return v

def low_keep(v):
    return (low(v), None)

def low_pass(kept, grad):
    return (grad,)

def back_keep(v):
    return (v, None)

def back_low(kept, grad):
    return (low(grad),)
low.defvjp(low_keep, low_pass)
low_back.defvjp(back_keep, back_low)
ln_eps = 1e-06
mask_fill = -1000000000.0
decay = 0.5
matrix_rate = 1.0
vector_rate = 0.1
vec_eps = 1e-12
highest = lax.Precision.HIGHEST

def matrix_shapes():
    return ((D, 3 * D), (D, D), (D, FF), (FF, D))

def to_matrix(blocks, height, extent):
    block_size = blocks.shape[-1]
    return blocks.reshape(height // block_size, extent // block_size, block_size, block_size).transpose(0, 2, 1, 3).reshape(height, extent)

def to_blocks(matrix, block_size):
    height, extent = matrix.shape
    return matrix.reshape(height // block_size, block_size, extent // block_size, block_size).transpose(0, 2, 1, 3).reshape(-1, block_size, block_size)

def assemble(all_blocks, owner_slot):
    block_size = all_blocks.shape[-1]
    picked = jnp.take(all_blocks, owner_slot, axis=0)
    matrices = []
    offset = 0
    for height, extent in matrix_shapes():
        number = height // block_size * (extent // block_size)
        matrices.append(to_matrix(picked[offset:offset + number], height, extent))
        offset = offset + number
    return tuple(matrices)

def split_vectors(packed):
    extents = (D, D, D, D, D, FF, D, D, D)
    pieces = []
    offset = 0
    for extent in extents:
        pieces.append(packed[offset:offset + extent])
        offset = offset + extent
    return pieces

def matmul(left, right):
    return jnp.dot(left, right, precision=highest, preferred_element_type=jnp.float32)

def layer_norm(hidden, gain_vec, shift_vec):
    center = hidden - lax.optimization_barrier(jnp.mean(hidden, axis=-1, keepdims=True))
    spread = lax.optimization_barrier(jnp.mean(center * center, axis=-1, keepdims=True))
    return center * lax.rsqrt(spread + ln_eps) * gain_vec + shift_vec

def forward(matrices, packed, tokens, lens):
    w_qkv, w_out, w_up, w_down = [low(m) for m in matrices]
    b_q, b_v, b_o, g_one, s_one, b_up, b_down, g_two, s_two = split_vectors(low(packed))
    count = lens.shape[0]
    seq_len = tokens.shape[0] // count
    bias_qkv = jnp.concatenate([b_q, jnp.zeros_like(b_q), b_v])
    qkv = low(low_back(matmul(tokens, w_qkv) + bias_qkv))
    queries = qkv[:, :D].reshape(count, seq_len, HEADS, HEAD)
    keys = qkv[:, D:2 * D].reshape(count, seq_len, HEADS, HEAD)
    values = qkv[:, 2 * D:].reshape(count, seq_len, HEADS, HEAD)
    scores = low_back(jnp.einsum('gqhd,gkhd->ghqk', queries, keys, precision=highest) * HEAD ** (-0.5))
    key_live = jnp.arange(seq_len)[None, :] < lens[:, None]
    scores = jnp.where(key_live[:, None, None, :], scores, mask_fill)
    probs = low(jax.nn.softmax(scores, axis=-1))
    mixed = jnp.einsum('ghqk,gkhd->gqhd', probs, values, precision=highest).reshape(count * seq_len, D)
    mixed = low(low_back(mixed))
    att_lin = low_back(matmul(mixed, w_out) + b_o)
    y_one = layer_norm(tokens + att_lin, g_one, s_one)
    z_up = low_back(matmul(low(y_one), w_up) + b_up)
    act = low(jax.nn.gelu(z_up, approximate=False))
    z_down = low_back(matmul(act, w_down) + b_down)
    return layer_norm(y_one + z_down, g_two, s_two)

def reference(inputs, cotangent, lengths, owner_slot, weights, vectors, left_stat, right_stat, left_root, right_root, vector_stat):
    block_size = weights.shape[-1]
    matrices = assemble(weights, owner_slot)
    group = math.gcd(SEQS, max(1, 4096 // MAXLEN))
    turns = SEQS // group
    tok_groups = inputs.reshape(turns, group * MAXLEN, D)
    cot_groups = cotangent.reshape(turns, group * MAXLEN, D)
    len_groups = lengths.reshape(turns, group)

    def one_group(carry, batch):
        tokens_g, cot_g, lens_g = batch
        valid = (jnp.arange(MAXLEN)[None, :] < lens_g[:, None]).reshape(-1)
        result, pull = jax.vjp(lambda mats, packed, tokens: forward(mats, packed, tokens, lens_g), matrices, vectors, tokens_g.astype(vectors.dtype))
        grad_mats, grad_vec, grad_tok = pull(cot_g.astype(vectors.dtype) * valid[:, None].astype(vectors.dtype))
        summed = tuple((a + b for a, b in zip(carry[0], grad_mats)))
        return ((summed, carry[1] + grad_vec), (result.astype(jnp.bfloat16), grad_tok.astype(jnp.bfloat16)))
    init = (tuple((jnp.zeros_like(m) for m in matrices)), jnp.zeros_like(vectors))
    (grad_mats, vector_grads), (result, grad_tok) = lax.scan(one_group, init, (tok_groups, cot_groups, len_groups))
    outputs = result.reshape(TOKENS, D)
    input_grad = grad_tok.reshape(TOKENS, D)
    block_list = jnp.concatenate([to_blocks(m, block_size) for m in grad_mats], axis=0)
    block_grads = jnp.zeros_like(weights).at[owner_slot].set(block_list)
    new_left = decay * left_stat + (1.0 - decay) * jnp.einsum('sij,skj->sik', block_grads, block_grads, precision=highest)
    new_right = decay * right_stat + (1.0 - decay) * jnp.einsum('sji,sjk->sik', block_grads, block_grads, precision=highest)
    inner = jnp.einsum('sij,sjk->sik', block_grads, right_root, precision=highest)
    step = jnp.einsum('sij,sjk->sik', left_root, inner, precision=highest)
    new_weights = weights - matrix_rate * step
    new_vector_stat = decay * vector_stat + (1.0 - decay) * vector_grads * vector_grads
    new_vectors = vectors - vector_rate * vector_grads * lax.rsqrt(new_vector_stat + vec_eps)
    return (outputs, input_grad, block_grads, new_left, new_right, new_weights, vector_grads, new_vector_stat, new_vectors)
```

```python
import functools
import math

import jax
import jax.numpy as jnp
from jax import lax
from jax.experimental import pallas as pl
from jax.experimental.pallas import tpu as pltpu
from jax.sharding import PartitionSpec as P

D = 768
HEADS = 12
HEAD = 64
FF = 3072
BLK = 256
HALF = BLK // 2
TAIL = 16
LANES = 128
TILE = 16
TILES = HALF // TILE
LN_EPS = 1e-06
FILL = -1000000000.0
VEC_EPS = 1e-12
SCALE = HEAD ** (-0.5)
MIB = 1024 * 1024
WIDE = 1024

f32 = jnp.float32
bf16 = jnp.bfloat16
MESH = pl.DeviceIdType.MESH
VMEM = pltpu.VMEM
SMEM = pltpu.SMEM

QKV_AT, OUT_AT, UP_AT, DOWN_AT, ALL = 0, 27, 36, 72, 108
REST_ROWS, QKV_ROWS = (ALL - OUT_AT) * TILE, OUT_AT * TILE
GROUP_ROWS = QKV_ROWS // 3

B_Q, B_V, B_O, G_ONE, S_ONE, B_UP, B_DOWN, G_TWO, S_TWO = (
    0, 768, 1536, 2304, 3072, 3840, 6912, 7680, 8448)

LATE_Z = (False, False, True, True, True, True)
STEPS = (
    (),
    (),
    (),
    ("0b2",),
    ("0b6", "1b3",),
    ("0b4", "0b3", "1b5",),
    ("2b0",),
    ("0b0", "0z3", "1b2", "0b5", "1z3",),
    ("1b4", "0z0",),
    ("2a0", "1z2", "1b1",),
    ("2b3", "2b4", "2b6", "1b0", "3b3", "3b2", "0z2", "3b5", "2b1",),
    ("1z1", "4b3", "2a3", "1w1",),
    ("1b6", "4b1", "3b0", "1w0", "2b5", "4b0",),
    ("1z0", "0b7",),
    ("0w0", "3b1", "2a1", "0b1", "0w1",),
    ("4b5", "4b2", "2z0", "4a1", "3a0", "2z1", "3b4", "2b2", "1a0",),
    ("3a1", "5b1", "0z1", "5b3", "4a0", "5b0", "v0", "5b4", "4b4", "5b2", "4a2",),
    ("v1", "5b5", "5a1", "4z1", "2a2", "4b6", "3z0", "3z1", "0a0", "1b7", "v2", "5a0", "3a2", "4z0", "3b6",
     "5a2", "5z1", "5b6", "2w0", "4w0", "3a3",),
    ("v3", "5b7", "2b7", "5a3", "3b7", "5z0", "5w0", "4b7", "4a3", "3w0", "0f", "2f", "1f", "v4", "5f", "4f",
     "3f", "v5",),
)


def dot(a, b):
    return lax.dot_general(a, b, (((1,), (0,)), ((), ())), preferred_element_type=f32)


def dot_nt(a, b):
    return lax.dot_general(a, b, (((1,), (1,)), ((), ())), preferred_element_type=f32)


def dot_tn(a, b):
    return lax.dot_general(a, b, (((0,), (0,)), ((), ())), preferred_element_type=f32)


def cols(index, width):
    return pl.ds(pl.multiple_of(index * width, width), width)


def fetch(slot_ref, w_hbm, buf, sem, block, row, col, per):
    slot = slot_ref[block]
    at = pl.multiple_of((slot % per) * TILES, TILES)
    return pltpu.make_async_copy(
        w_hbm.at[slot // per, :, pl.ds(at, TILES), :, :],
        buf.at[pl.ds(2 * row, 2), :, :, cols(col, BLK)],
        sem,
    )


def put(buf, g_hbm, sems, n, row, col):
    for half in range(2):
        yield pltpu.make_async_copy(
            buf.at[pl.ds(2 * row, 2), :, :, pl.ds(col * BLK + half * LANES, LANES)],
            g_hbm.at[half, :, :, pl.ds(n * TILE, TILE), :],
            sems.at[2 * n + half],
        )


def panel(buf, col, width):
    got = buf[:, :, :, cols(col, width)]
    return got.reshape(got.shape[0] * HALF, width)


def front_kernel(per, seq, slot, lens, x_hbm, w_hbm, vec, qkv_out, mixed_out, lse_out, wq_out, x, qkv, mixed, lse, wbuf, even, odd, sems, io_sems):
    def copy(block):
        return fetch(slot, w_hbm, wbuf, sems.at[block], QKV_AT + block, block // 9, block % 9, per)

    def in_part(part):
        return [copy(row * 9 + 3 * part + col) for row in range(3) for col in range(3)]

    load_x = pltpu.make_async_copy(x_hbm, x, io_sems.at[0])
    load_x.start()
    for part in range(3):
        for c in in_part(part):
            c.start()
    load_x.wait()
    saves = []
    for part in range(3):
        for c in in_part(part):
            c.wait()
        at = slice(part * D, (part + 1) * D)
        got = dot(x[...], wbuf[:, :, :, at].reshape(D, D))
        if part != 1:
            bias = B_Q if part == 0 else B_V
            got = got + vec[:, bias:bias + D]
        qkv[:, at] = got.astype(bf16)
        saves.append(pltpu.make_async_copy(qkv.at[:, at], qkv_out.at[:, at], io_sems.at[1 + part]))
        saves[-1].start()
    saves.append(pltpu.make_async_copy(wbuf, wq_out, io_sems.at[8]))
    saves[-1].start()

    lane = lax.broadcasted_iota(jnp.int32, (seq, 2 * HEAD), 1)
    key = lax.broadcasted_iota(jnp.int32, (1, seq), 1)

    def where(item):
        sent, pair = item // 6, item % 6
        return sent, pair, pl.ds(pl.multiple_of(sent * seq, seq), seq)

    def score(item, buf):
        sent, pair, rows = where(item)
        q = qkv[rows, cols(pair, 128)] * SCALE
        k = qkv[rows, cols(6 + pair, 128)]
        two = jnp.concatenate([jnp.where(lane < HEAD, q, 0), jnp.where(lane >= HEAD, q, 0)], axis=0)
        buf[...] = dot_nt(two, k)

    def attend(item, buf):
        sent, pair, rows = where(item)
        v = qkv[rows, cols(12 + pair, 128)]
        scores = jnp.where(key < lens[sent], buf[...], FILL)
        top = jnp.max(scores, axis=-1, keepdims=True)
        expo = jnp.exp(scores - top).astype(bf16)
        values = [
            jnp.concatenate([jnp.where((lane < HEAD) == (h == 0), v, 0), jnp.where(lane == h, 1, 0).astype(bf16)], axis=1)
            for h in range(2)
        ]
        got = dot(jnp.concatenate([expo[:seq], expo[seq:]], axis=1), jnp.concatenate(values, axis=0))
        sums = got[:, 128:130]
        inverse = 1.0 / sums
        mixed[rows, cols(pair, 128)] = (
            got[:, :128] * jnp.where(lane < HEAD, inverse[:, 0:1], inverse[:, 1:2])).astype(bf16)
        logs = jnp.log(sums)
        kept = jnp.where(lane == 2 * pair, top[:seq] + logs[:, 0:1], lse[rows, :])
        lse[rows, :] = jnp.where(lane == 2 * pair + 1, top[seq:] + logs[:, 1:2], kept)

    def both(i, carry):
        score(2 * i + 1, odd)
        attend(2 * i, even)
        score(jnp.minimum(2 * i + 2, 11), even)
        attend(2 * i + 1, odd)
        return carry

    lse[...] = jnp.zeros_like(lse)
    score(0, even)
    for sent in range(x.shape[0] // seq):
        lax.fori_loop(3 * sent, 3 * sent + 3, both, 0)
        rows = pl.ds(sent * seq, seq)
        for n, (src, dst) in enumerate(((mixed, mixed_out), (lse, lse_out))):
            saves.append(pltpu.make_async_copy(src.at[rows, :], dst.at[rows, :], io_sems.at[4 + 2 * sent + n]))
            saves[-1].start()
    for c in saves:
        c.wait()


def front(slot, lens, x, w_all, vec, per):
    tok = x.shape[0]
    seq = tok // lens.shape[0]
    any_spec = pl.BlockSpec(memory_space=pl.ANY)
    smem, vmem = pl.BlockSpec(memory_space=SMEM), pl.BlockSpec(memory_space=VMEM)
    return pl.pallas_call(
        functools.partial(front_kernel, per, seq),
        out_shape=(
            jax.ShapeDtypeStruct((tok, 3 * D), bf16),
            jax.ShapeDtypeStruct((tok, D), bf16),
            jax.ShapeDtypeStruct((tok, 128), f32),
            jax.ShapeDtypeStruct((6, TILES, TILE, 3 * D), bf16),
        ),
        in_specs=[smem, smem, any_spec, any_spec, vmem],
        out_specs=(any_spec,) * 4,
        scratch_shapes=[
            VMEM((tok, D), bf16), VMEM((tok, 3 * D), bf16), VMEM((tok, D), bf16), VMEM((tok, 128), f32),
            VMEM((6, TILES, TILE, 3 * D), bf16), VMEM((2 * seq, seq), f32), VMEM((2 * seq, seq), f32),
            pltpu.SemaphoreType.DMA((27,)), pltpu.SemaphoreType.DMA((9,)),
        ],
        compiler_params=pltpu.CompilerParams(vmem_limit_bytes=60 * MIB),
        name="front",
    )(slot, lens, x, w_all, vec)


def norm(hidden):
    center = hidden - jnp.mean(hidden, axis=-1, keepdims=True)
    spread = jnp.mean(center * center, axis=-1, keepdims=True)
    rstd = lax.rsqrt(spread + LN_EPS)
    return center * rstd, rstd


def norm_back(grad, normed, rstd, gain):
    scaled = grad * gain
    return rstd * (
        scaled
        - jnp.mean(scaled, axis=-1, keepdims=True)
        - normed * jnp.mean(scaled * normed, axis=-1, keepdims=True)
    )


def col_sum(a):
    return jnp.sum(a, axis=0, keepdims=True)


def gelu_and_slope(z):
    cdf = 0.5 + 0.5 * lax.erf(z * math.sqrt(0.5))
    density = jnp.exp2(z * z * (-0.5 / math.log(2.0))) * (1.0 / math.sqrt(2.0 * math.pi))
    return z * cdf, cdf + z * density


def middle_kernel(
    per, seq, slot, lens, x_hbm, cot_hbm, mixed_hbm, vec, w_hbm,
    outputs_hbm, d_one_hbm, d_mixed_hbm, vgrad, g_hbm,
    x, cot, mixed, outputs, d_one_out, d_mixed,
    w_out, w_up, w_down, act, y_low, dz_up, dz_down, slope, h_buf, n_buf, sems, put_sems, in_sems, out_sems,
):
    tok = x.shape[0]
    places = (
        [(OUT_AT + i, w_out, i // 3, i % 3) for i in range(9)]
        + [(UP_AT + i, w_up, i // 12, i % 12) for i in range(36)]
        + [(DOWN_AT + i, w_down, i // 3, i % 3) for i in range(36)]
    )

    def copies(kind, lo, hi):
        for block, buf, row, col in places:
            if lo <= block < hi:
                if kind == "get":
                    yield fetch(slot, w_hbm, buf, sems.at[block - OUT_AT], block, row, col, per)
                else:
                    yield from put(buf, g_hbm, put_sems, block - OUT_AT, row, col)

    def first(sent, lo, hi):
        @pl.when(sent == 0)
        def _():
            for c in copies("get", lo, hi):
                c.wait()

    loads = [
        pltpu.make_async_copy(src, dst, in_sems.at[n])
        for n, (src, dst) in enumerate(((mixed_hbm, mixed), (x_hbm, x), (cot_hbm, cot)))
    ]
    loads[0].start()
    for c in copies("get", OUT_AT, UP_AT):
        c.start()
    loads[1].start()
    for c in copies("get", UP_AT, 108):
        c.start()
    loads[2].start()

    def save(n, src, dst, sent):
        rows = pl.ds(pl.multiple_of(sent * seq, seq), seq)
        return pltpu.make_async_copy(src.at[rows, :], dst.at[rows, :], out_sems.at[n, sent])

    def vec_at(at, width=D):
        return vec[:, at:at + width]

    def vadd(at, value):
        for t in range(value.shape[1] // LANES):
            row = (at - B_O) // LANES + t
            vgrad[row:row + 1, :] += value[:, t * LANES:(t + 1) * LANES]

    vgrad[...] = jnp.zeros_like(vgrad)

    def tile(sent, carry):
        rows = pl.ds(pl.multiple_of(sent * seq, seq), seq)
        first(sent, OUT_AT, UP_AT)

        @pl.when(sent == 0)
        def _():
            loads[0].wait()
            loads[1].wait()

        att = dot(mixed[rows, :], w_out[...].reshape(D, D)) + vec_at(B_O)
        n_one, r_one = norm(x[rows, :].astype(f32) + att)
        n_buf[...] = n_one
        y_one = n_one * vec_at(G_ONE) + vec_at(S_ONE)
        h_buf[...] = y_one
        y_low[rows, :] = y_one.astype(bf16)
        first(sent, UP_AT, DOWN_AT)

        for j in range(FF // WIDE):
            at = slice(j * WIDE, (j + 1) * WIDE)
            z = dot(y_low[rows, :], panel(w_up, j, WIDE)) + vec_at(B_UP + j * WIDE, WIDE)
            got, got_slope = gelu_and_slope(z)
            act[rows, at] = got.astype(bf16)
            slope[:, at] = got_slope
        first(sent, DOWN_AT, 108)

        @pl.when(sent == 0)
        def _():
            loads[2].wait()


        z_down = dot(act[rows, :], w_down[...].reshape(FF, D)) + vec_at(B_DOWN)
        n_two, r_two = norm(h_buf[...] + z_down)
        outputs[rows, :] = (n_two * vec_at(G_TWO) + vec_at(S_TWO)).astype(bf16)
        save(0, outputs, outputs_hbm, sent).start()

        live = lax.broadcasted_iota(jnp.int32, (seq, 1), 0) < lens[sent]
        grad = jnp.where(live, cot[rows, :].astype(f32), 0.0)
        vadd(G_TWO, col_sum(grad * n_two))
        vadd(S_TWO, col_sum(grad))
        d_two = norm_back(grad, n_two, r_two, vec_at(G_TWO))
        h_buf[...] = d_two
        low = d_two.astype(bf16)
        dz_down[rows, :] = low
        vadd(B_DOWN, col_sum(low.astype(f32)))

        for j in range(FF // WIDE):
            at = slice(j * WIDE, (j + 1) * WIDE)
            w = w_down[j * WIDE // HALF:(j + 1) * WIDE // HALF, :, :].reshape(WIDE, D)
            got = (dot_nt(dz_down[rows, :], w) * slope[:, at]).astype(bf16)
            dz_up[rows, at] = got
            vadd(B_UP + j * WIDE, col_sum(got.astype(f32)))

        d_y = h_buf[...] + dot_nt(dz_up[rows, :], w_up[...].reshape(D, FF))
        vadd(G_ONE, col_sum(d_y * n_buf[...]))
        vadd(S_ONE, col_sum(d_y))
        d_one = norm_back(d_y, n_buf[...], r_one, vec_at(G_ONE))
        d_one_out[rows, :] = d_one
        d_low = d_one.astype(bf16)
        vadd(B_O, col_sum(d_low.astype(f32)))
        d_mixed[rows, :] = dot_nt(d_low, w_out[...].reshape(D, D)).astype(bf16)
        save(1, d_one_out, d_one_hbm, sent).start()
        save(2, d_mixed, d_mixed_hbm, sent).start()
        return carry

    lax.fori_loop(0, tok // seq, tile, 0)

    for i in range(FF // WIDE):
        got = dot_tn(act[:, i * WIDE:(i + 1) * WIDE], dz_down[...])
        w_down[i * WIDE // HALF:(i + 1) * WIDE // HALF, :, :] = got.astype(bf16).reshape(WIDE // HALF, TILES, TILE, D)
        for c in copies("put", DOWN_AT + 12 * i, DOWN_AT + 12 * (i + 1)):
            c.start()
    for i in range(FF // WIDE):
        got = dot_tn(y_low[...], dz_up[:, i * WIDE:(i + 1) * WIDE])
        w_up[:, :, :, i * WIDE:(i + 1) * WIDE] = got.astype(bf16).reshape(6, TILES, TILE, WIDE)
        for row in range(3):
            for c in copies("put", UP_AT + 12 * row + 4 * i, UP_AT + 12 * row + 4 * (i + 1)):
                c.start()
    w_out[...] = dot_tn(mixed[...], d_one_out[...].astype(bf16)).astype(bf16).reshape(6, TILES, TILE, D)
    for c in copies("put", OUT_AT, UP_AT):
        c.start()
    for sent in range(tok // seq):
        save(0, outputs, outputs_hbm, sent).wait()
        save(1, d_one_out, d_one_hbm, sent).wait()
        save(2, d_mixed, d_mixed_hbm, sent).wait()
    for c in copies("put", OUT_AT, 108):
        c.wait()


def middle(slot, lens, x, cot, mixed, vec, w_all, per):
    tok = x.shape[0]
    seq = tok // lens.shape[0]
    any_spec = pl.BlockSpec(memory_space=pltpu.HBM)
    smem, vmem = pl.BlockSpec(memory_space=SMEM), pl.BlockSpec(memory_space=VMEM)
    return pl.pallas_call(
        functools.partial(middle_kernel, per, seq),
        out_shape=(
            jax.ShapeDtypeStruct((tok, D), bf16),
            jax.ShapeDtypeStruct((tok, D), f32),
            jax.ShapeDtypeStruct((tok, D), bf16),
            jax.ShapeDtypeStruct(((vec.shape[1] - B_O) // LANES, LANES), f32),
            jax.ShapeDtypeStruct((2, 2, TILES, REST_ROWS, LANES), bf16),
        ),
        in_specs=[smem, smem, any_spec, any_spec, any_spec, vmem, any_spec],
        out_specs=(any_spec, any_spec, any_spec, vmem, any_spec),
        scratch_shapes=[
            VMEM((tok, D), bf16),
            VMEM((tok, D), bf16),
            VMEM((tok, D), bf16),
            VMEM((tok, D), bf16),
            VMEM((tok, D), f32),
            VMEM((tok, D), bf16),
            VMEM((6, TILES, TILE, D), bf16),
            VMEM((6, TILES, TILE, FF), bf16),
            VMEM((24, TILES, TILE, D), bf16),
            VMEM((tok, FF), bf16),
            VMEM((tok, D), bf16),
            VMEM((tok, FF), bf16),
            VMEM((tok, D), bf16),
            VMEM((seq, FF), f32),
            VMEM((seq, D), f32),
            VMEM((seq, D), f32),
            pltpu.SemaphoreType.DMA((81,)),
            pltpu.SemaphoreType.DMA((162,)),
            pltpu.SemaphoreType.DMA((3,)),
            pltpu.SemaphoreType.DMA((3, tok // seq)),
        ],
        compiler_params=pltpu.CompilerParams(vmem_limit_bytes=63 * MIB),
        name="middle",
    )(slot, lens, x, cot, mixed, vec, w_all)


class Place:
    def __init__(self):
        chip = lax.axis_index("fsdp")
        self.core, self.me = lax.axis_index("dp"), chip
        z, y, x = chip // 4, (chip // 2) % 2, chip % 2
        core = self.core
        self.z, self.a, self.b = z, y * (1 - core) + x * core, x * (1 - core) + y * core
        self.near, self.mid, self.far = z + 1 - 2 * (z % 2), (z + 2) % 4, 3 - z
        self.index = z * 4 + self.a * 2 + self.b
        self.peer_a = core, self.chip(z, 1 - self.a, self.b)
        self.peer_b = core, self.chip(z, self.a, 1 - self.b)
        self.peer_z = core, self.chip(self.near, self.a, self.b)
        self.peer_w = core, self.chip(self.far, self.a, self.b)
        self.sibling = 1 - core, chip

    def chip(self, z, a, b):
        return z * 4 + a * (2 - self.core) + b * (1 + self.core)

    def at_index(self, index):
        return self.core, self.chip(index // 4, (index // 2) % 2, index % 2)

    def others(self):
        return [self.at_index((self.index + k) % 16) for k in range(1, 16)]

    def near_peers(self):
        return [self.peer_a, self.peer_b, self.peer_z, self.peer_w]

    def greet(self, peers):
        barrier = pltpu.get_barrier_semaphore()
        peers = peers + [self.sibling]
        for peer in peers:
            pl.semaphore_signal(barrier, inc=1, device_id=peer, device_id_type=MESH)
        pl.semaphore_wait(barrier, len(peers))


def remote(src, dst, send_sem, recv_sem, to):
    return pltpu.make_async_remote_copy(
        src_ref=src, dst_ref=dst, send_sem=send_sem, recv_sem=recv_sem, device_id=to, device_id_type=MESH)


def chunk_rows(total, parts, tile=16):
    tiles, first, got = total // tile, 0, []
    for i in range(parts):
        rows = (tiles // parts + (i < tiles % parts)) * tile
        got.append((first, rows))
        first += rows
    return got


def in_turns(lags, parts):
    for turn in range(parts + lags[-1]):
        for n, lag in enumerate(lags):
            if 0 <= turn - lag < parts:
                yield n, turn - lag


def gather_kernel(chunks, w, tail, out, own, keep_sem, send_sems, main_sems, sib_sems):
    p = Place()
    for i in range(w.shape[0]):
        own[:, i * HALF:(i + 1) * HALF, :] = w[i].astype(bf16).reshape(2, HALF, BLK)
    own[:, w.shape[0] * HALF:, :] = tail[...]
    p.greet(p.near_peers())
    keep = pltpu.make_async_copy(own, out.at[p.me], keep_sem)
    keep.start()
    sends = []
    a, b = p.a, p.b

    def window(i):
        return pl.ds(*chunks[i])

    def send(i, chip, *peers):
        src = own.at[p.core, window(i), :] if chip is p.me else out.at[chip, p.core, window(i), :]
        for to in peers:
            sems = sib_sems if to is p.sibling else main_sems
            c = pltpu.make_async_remote_copy(
                src_ref=src, dst_ref=out.at[chip, p.core, window(i), :],
                send_sem=send_sems.at[len(sends)], recv_sem=sems.at[i, chip], device_id=to, device_id_type=MESH)
            c.start()
            sends.append(c)

    def arrive(i, chip, half, sems):
        there = out.at[chip, half, window(i), :]
        pltpu.make_async_remote_copy(
            src_ref=there, dst_ref=there, send_sem=send_sems.at[0], recv_sem=sems.at[i, chip],
            device_id=p.sibling, device_id_type=MESH).wait_recv()

    def forward(i, chip, *peers):
        arrive(i, chip, p.core, main_sems)
        send(i, chip, *peers, p.sibling)

    def stage(n, i):
        z_first = i == 0
        if n == 0 and z_first:
            forward(i, p.chip(p.far, a, b), p.peer_z, p.peer_a, p.peer_b)
        elif n == 1 and z_first:
            for zz in (p.near, p.mid):
                forward(i, p.chip(zz, a, b), p.peer_a, p.peer_b)
        elif n == 2 and z_first:
            for zz in (p.z, p.far, p.near, p.mid):
                forward(i, p.chip(zz, 1 - a, b), p.peer_b)
        elif n == 0:
            forward(i, p.chip(p.z, 1 - a, b), p.peer_w, p.peer_z, p.peer_b)
        elif n == 1:
            for aa in (a, 1 - a):
                forward(i, p.chip(p.far, aa, b), p.peer_z, p.peer_b)
        elif n == 2:
            for zz in (p.near, p.mid):
                for aa in (a, 1 - a):
                    forward(i, p.chip(zz, aa, b), p.peer_b)
        else:
            for zz in (p.z, p.far, p.near, p.mid):
                for aa in (a, 1 - a):
                    forward(i, p.chip(zz, aa, 1 - b))

    for i in range(len(chunks)):
        if i == 0:
            send(i, p.me, p.peer_w, p.peer_z, p.peer_a, p.peer_b)
        else:
            send(i, p.me, p.peer_a, p.peer_w, p.peer_z, p.peer_b)
    for n, i in in_turns((0, 2, 3, 4), len(chunks)):
        stage(n, i)
    for i in range(len(chunks)):
        for k in range(1, 16):
            arrive(i, (p.me + k) % 16, 1 - p.core, sib_sems)
    for c in sends:
        c.wait_send()
    keep.wait()


def gather(weights, tail):
    shape = (2, weights.shape[0] * HALF + TAIL, BLK)
    chunks = chunk_rows(shape[1], 3)
    vmem = pl.BlockSpec(memory_space=VMEM)
    dma = pltpu.SemaphoreType.DMA
    return pl.pallas_call(
        functools.partial(gather_kernel, chunks),
        out_shape=jax.ShapeDtypeStruct((16,) + shape, bf16),
        in_specs=[vmem, vmem],
        out_specs=pl.BlockSpec(memory_space=pl.ANY),
        scratch_shapes=[
            VMEM(shape, bf16), dma, dma((30 * len(chunks),)), dma((len(chunks), 16)), dma((len(chunks), 16))],
        compiler_params=pltpu.CompilerParams(
            collective_id=1, has_side_effects=True, vmem_limit_bytes=60 * MIB),
        name="gather",
    )(weights, tail)


class Sums:
    def __init__(self, place, chunks, late_z, ready, mine, sib, got_b, got_a, got_z, got_w, result, send_sems, recv_sems):
        self.p, self.chunks, self.late_z, self.ready = place, chunks, late_z, ready
        self.mine, self.sib, self.result = mine, sib, result
        self.got = {"b": got_b, "a": got_a, "z": got_z, "w": got_w}
        self.send_sems, self.recv_sems = send_sems, recv_sems
        self.begun = set()

    def shard(self, i, name):
        p, k = self.p, int(name[1:] or 0)
        zs, sides = (p.near, p.mid, p.far, p.z), (1 - p.a, p.a)
        if self.late_z[i]:
            order = [(z, a) for a in sides for z in zs]
            first = {"b": 0, "a": 0, "z": 4, "w": 6, "f": 7}[name[0]]
        else:
            order = [(z, a) for z in zs for a in sides]
            first = {"b": 0, "z": 0, "w": 4, "a": 6, "f": 7}[name[0]]
        return (*order[first + k], 1 - p.b if name[0] == "b" else p.b)

    def parts(self, i, name):
        k = int(name[1:] or 0)
        if self.late_z[i]:
            return {
                "b": (), "a": (f"b{k}",), "z": (f"b{4 + k}", f"a{k}"), "w": ("b6", "a2", "z1"),
                "f": ("b7", "a3", "z0", "w0")}[name[0]]
        return {
            "b": (), "z": (f"b{k}",), "w": (f"b{4 + k}", f"z{2 + k}"), "a": ("b6", "z0", "w0"),
            "f": ("b7", "z1", "w1", "a0")}[name[0]]

    def names(self, i):
        rest = ("a0", "a1", "a2", "a3", "z0", "z1", "w0") if self.late_z[i] else ("z0", "z1", "z2", "z3", "w0", "w1", "a0")
        return [f"b{k}" for k in range(8)] + list(rest)

    def copy(self, i, name):
        p = self.p
        at = pl.ds(*self.chunks[i])
        to = {"b": p.peer_b, "a": p.peer_a, "z": p.peer_z, "w": p.peer_w}[name[0]]
        n = self.names(i).index(name)
        return remote(
            self.mine.at[(*self.shard(i, name), at, slice(None))],
            self.got[name[0]].at[int(name[1:]), at, :],
            self.send_sems.at[i, n], self.recv_sems.at[i, n], to)

    def step(self, i, name):
        if i not in self.begun:
            self.begun.add(i)
            self.ready(i)
        parts = self.parts(i, name)
        for part in parts:
            self.copy(i, part).wait_recv()
        where = self.shard(i, name)
        lo, number = self.chunks[i]

        def add(n, carry):
            at = pl.ds(pl.multiple_of(lo + n * GROUP_ROWS, TILE), GROUP_ROWS)
            here = (*where, at, slice(None))
            if not parts:
                self.mine[here] = self.mine[here] + self.sib[here]
                return carry
            acc = self.mine[here].astype(f32) + self.sib[here].astype(f32)
            for part in parts:
                acc = acc + self.got[part[0]][int(part[1:]), at, :].astype(f32)
            low = acc.astype(bf16)
            if name == "f":
                blocks = GROUP_ROWS // TILE
                self.result[pl.ds(lo // TILE + n * blocks, blocks), :, :] = low.reshape(blocks, TILE, LANES)
            else:
                self.mine[here] = low
            return carry

        lax.fori_loop(0, number // GROUP_ROWS, add, 0)
        if name != "f":
            self.copy(i, name).start()

    def end(self):
        for i in range(len(self.chunks)):
            for name in self.names(i):
                self.copy(i, name).wait_send()


def rear_kernel(comm, per, seq, lens, x_hbm, qkv_hbm, d_mixed_hbm, lse, d_one_hbm, wq, *refs):
    tok = x_hbm.shape[0]
    if comm:
        (
            g_rest, vg_rest, inverse, input_grad_hbm, vec_sum, owned,
            x, qkv, d_mixed, d_one, input_grad, wbuf, d_qkv, lse_t, in_sems, out_sems,
            mine, sib, got_b, got_a, got_z, got_w, give, result, picked, g_own, g_sib, vec_got,
            keep_sems, sib_send, sib_recv, rs_send, rs_recv, xs_send, xs_recv, pair_sems, vec_send, vec_recv,
        ) = refs
        p = Place()
        p.greet(p.others())
        chunks = [(i * QKV_ROWS, QKV_ROWS) for i in range(3)] + [(REST_ROWS + g * GROUP_ROWS, GROUP_ROWS) for g in range(3)]

        def sib_copy(i):
            at = pl.ds(*chunks[i])
            if i < 3:
                src = g_rest.at[1 - p.core, :, :, :, at, :]
            else:
                src = give.at[:, :, :, pl.ds((i - 3) * GROUP_ROWS, GROUP_ROWS), :]
            return remote(src, sib.at[:, :, :, at, :], sib_send.at[i], sib_recv.at[i], p.sibling)

        def keep(i):
            at = pl.ds(*chunks[i])
            return pltpu.make_async_copy(g_rest.at[p.core, :, :, :, at, :], mine.at[:, :, :, at, :], keep_sems.at[i])

        def ready(i):
            if i < 3:
                keep(i).wait()
            sib_copy(i).wait_recv()

        for i in range(3):
            sib_copy(i).start()
            keep(i).start()
        sums = Sums(
            p, chunks, LATE_Z, ready, mine, sib, got_b, got_a, got_z, got_w, result, rs_send, rs_recv)
        chip = lax.axis_index("fsdp")
        z, y, x_at = chip // 4, (chip // 2) % 2, chip % 2
        hops = (
            p.sibling, (p.core, z * 4 + y * 2 + 1 - x_at), (p.core, z * 4 + (1 - y) * 2 + x_at), p.peer_z, p.peer_w)

        def vec_copy(n):
            return remote(vec_got.at[2 * n], vec_got.at[2 * n + 1], vec_send.at[n], vec_recv.at[n], hops[n])

        def vec_step(n):
            if n > 0:
                vec_copy(n - 1).wait_recv()
                vec_sum[...] = vec_sum[...] + vec_got[2 * n - 1]
            if n < 5:
                vec_got[2 * n] = vec_sum[...]
                vec_copy(n).start()

        def after(step):
            for name in STEPS[step + 1]:
                if name[0] == "v":
                    vec_step(int(name[1:]))
                else:
                    sums.step(int(name[0]), name[1:])
    else:
        (
            input_grad_hbm, vec_sum, g_qkv,
            x, qkv, d_mixed, d_one, input_grad, wbuf, d_qkv, lse_t, in_sems, out_sems, gbuf, put_sems,
        ) = refs

        def after(step):
            pass

    def load(sent):
        rows = pl.ds(sent * seq, seq)
        yield pltpu.make_async_copy(qkv_hbm.at[rows, :], qkv.at[rows, :], in_sems.at[2 * sent])
        yield pltpu.make_async_copy(d_mixed_hbm.at[rows, :], d_mixed.at[rows, :], in_sems.at[2 * sent + 1])

    later = [
        pltpu.make_async_copy(src, dst, in_sems.at[2 * (tok // seq) + n])
        for n, (src, dst) in enumerate(((x_hbm, x), (d_one_hbm, d_one), (wq, wbuf)))
    ]
    for sent in range(tok // seq):
        for c in load(sent):
            c.start()
    for c in later:
        c.start()

    lse_t[...] = lse[...].T
    lane = lax.broadcasted_iota(jnp.int32, (seq, 2 * HEAD), 1)
    key = lax.broadcasted_iota(jnp.int32, (seq, 1), 0)

    def stack(m):
        return jnp.concatenate([jnp.where(lane < HEAD, m, 0), jnp.where(lane >= HEAD, m, 0)], axis=0)

    def attend(sent, pair):
        rows = pl.ds(pl.multiple_of(sent * seq, seq), seq)
        q = qkv[rows, cols(pair, 128)] * SCALE
        k = qkv[rows, cols(6 + pair, 128)]
        v = qkv[rows, cols(12 + pair, 128)]
        go = d_mixed[rows, cols(pair, 128)]
        q_two, go_two, k_two = stack(q), stack(go), stack(k * SCALE)
        scores = jnp.where(key < lens[sent], dot_nt(k, q_two), FILL)
        logs = jnp.concatenate([lse_t[pl.ds(2 * pair + h, 1), rows] for h in range(2)], axis=1)
        probs = jnp.exp(scores - logs)
        d_probs = dot_nt(v, go_two)
        delta = jnp.sum(probs * d_probs, axis=0, keepdims=True)
        d_scores = (probs * (d_probs - delta)).astype(bf16)
        d_qkv[rows, cols(12 + pair, 128)] = dot(probs.astype(bf16), go_two).astype(bf16)
        d_qkv[rows, cols(6 + pair, 128)] = dot(d_scores, q_two).astype(bf16)
        turned = jnp.concatenate([d_scores[:, :seq], d_scores[:, seq:]], axis=0)
        d_qkv[rows, cols(pair, 128)] = dot_tn(turned, k_two).astype(bf16)

    def w_grad(g):
        at = [slice(part * D + g * BLK, part * D + (g + 1) * BLK) for part in range(3)]
        got = dot_tn(x[...], jnp.concatenate([d_qkv[:, a] for a in at], axis=1)).astype(bf16)
        for r in range(3):
            for part in range(3):
                block = got[r * BLK:(r + 1) * BLK, part * BLK:(part + 1) * BLK]
                if not comm:
                    gbuf[2 * r:2 * r + 2, :, :, at[part]] = block.reshape(2, TILES, TILE, BLK)
                    continue
                low, high = (
                    block[:, half * LANES:(half + 1) * LANES].reshape(4, 2, 2, TILE, LANES) for half in range(2))
                row = g * GROUP_ROWS + (3 * r + part) * TILE
                mine[:, :, :, REST_ROWS + row:REST_ROWS + row + TILE, :] = jnp.where(p.core == 0, low, high)
                give[:, :, :, row:row + TILE, :] = jnp.where(p.core == 0, high, low)
        if comm:
            sib_copy(3 + g).start()

    after(-1)
    for c in load(0):
        c.wait()
    for c in load(1):
        c.wait()
    for g in range(3):

        def item(n, carry):
            attend(n // 2, 2 * g + n % 2)
            if comm:
                for k in range(4):

                    @pl.when(n == k)
                    def _():
                        after(5 * g + k)
            return carry

        lax.fori_loop(0, 4, item, 0)
        if g == 0:
            later[0].wait()
        w_grad(g)
        after(5 * g + 4)

    for first, third in ((0, 0), (D // LANES, 2)):
        total = col_sum(d_qkv[:, third * D:(third + 1) * D].astype(f32))
        for t in range(D // LANES):
            vec_sum[first + t:first + t + 1, :] = total[:, t * LANES:(t + 1) * LANES]
    if comm:
        vec_sum[2 * D // LANES:, :] = vg_rest[...]
    else:
        puts = [c for n in range(27) for c in put(gbuf, g_qkv, put_sems, n, n // 9, n % 9)]
        for c in puts:
            c.start()
    after(15)

    later[1].wait()
    later[2].wait()
    saves = []
    for sent in range(tok // seq):
        rows = slice(sent * seq, (sent + 1) * seq)
        got = dot_nt(d_qkv[rows, :], wbuf[...].reshape(D, 3 * D)) + d_one[rows, :]
        input_grad[rows, :] = got.astype(bf16)
        saves.append(pltpu.make_async_copy(input_grad.at[rows, :], input_grad_hbm.at[rows, :], out_sems.at[sent]))
        saves[-1].start()
        after(16 + sent)
    for c in saves:
        c.wait()
    if not comm:
        for c in puts:
            c.wait()
        return

    def pick(s, carry):
        block = inverse[s]
        rows = result[jnp.maximum(block, 0)]
        picked[s // per, s % per] = jnp.where(block >= 0, rows, jnp.zeros_like(rows))
        return carry

    lax.fori_loop(0, 16 * per, pick, 0)

    def exchange(k, source):
        there = (p.index + k) % 16
        return remote(picked.at[there], g_own.at[source], xs_send.at[k], xs_recv.at[source], p.at_index(there))

    for k in range(1, 16):
        exchange(k, p.index).start()
    g_own[p.index] = picked[p.index]
    for k in range(1, 16):
        exchange(k, (p.index + k) % 16).wait_recv()
    pair = remote(g_own, g_sib, pair_sems.at[0], pair_sems.at[1], p.sibling)
    pair.start()
    pair.wait_recv()
    for s in range(per):
        here, there = g_own[:, s], g_sib[:, s]
        owned[s, :, :LANES] = jnp.where(p.core == 0, here, there).reshape(BLK, LANES)
        owned[s, :, LANES:] = jnp.where(p.core == 0, there, here).reshape(BLK, LANES)
    pair.wait_send()
    for k in range(1, 16):
        exchange(k, p.index).wait_send()
    for n in range(5):
        vec_copy(n).wait_send()
    for i in range(6):
        sib_copy(i).wait_send()
    sums.end()


def rear(lens, x, qkv, d_mixed, lse, d_one, wq, g_rest=None, vg_rest=None, inverse=None, per=0):
    tok = x.shape[0]
    seq = tok // lens.shape[0]
    hbm = pl.BlockSpec(memory_space=pl.ANY)
    smem, vmem = pl.BlockSpec(memory_space=SMEM), pl.BlockSpec(memory_space=VMEM)
    dma = pltpu.SemaphoreType.DMA
    comm = g_rest is not None
    args = (lens, x, qkv, d_mixed, lse, d_one, wq)
    in_specs = [smem, hbm, hbm, hbm, vmem, hbm, hbm]
    out_shape, out_specs = (jax.ShapeDtypeStruct((tok, D), bf16),), (hbm,)
    scratch = [
        VMEM((tok, D), bf16), VMEM((tok, 3 * D), bf16), VMEM((tok, D), bf16), VMEM((tok, D), f32), VMEM((tok, D), bf16),
        VMEM((6, TILES, TILE, 3 * D), bf16), VMEM((tok, 3 * D), bf16), VMEM((128, tok), f32),
        dma((2 * (tok // seq) + 3,)), dma((tok // seq,)),
    ]
    if comm:
        args += (g_rest.reshape(2, 4, 2, 2, REST_ROWS, LANES), vg_rest, inverse)
        in_specs += [hbm, vmem, smem]
        out_shape += (
            jax.ShapeDtypeStruct((vg_rest.shape[0] + 2 * D // LANES, LANES), f32),
            jax.ShapeDtypeStruct((per, BLK, BLK), bf16),
        )
        out_specs += (vmem, vmem)
        rows = REST_ROWS + QKV_ROWS
        blocks = VMEM((16, per, TILE, LANES), bf16)
        scratch += [
            VMEM((4, 2, 2, rows, LANES), bf16), VMEM((4, 2, 2, rows, LANES), bf16),
            VMEM((8, rows, LANES), bf16), VMEM((4, rows, LANES), bf16), VMEM((4, rows, LANES), bf16),
            VMEM((2, rows, LANES), bf16),
            VMEM((4, 2, 2, QKV_ROWS, LANES), bf16),
            VMEM((ALL, TILE, LANES), bf16),
            blocks, blocks, blocks,
            VMEM((10,) + out_shape[1].shape, f32),
            dma((3,)), dma((6,)), dma((6,)), dma((6, 15)), dma((6, 15)), dma((16,)), dma((16,)), dma((2,)),
            dma((5,)), dma((5,)),
        ]
        params = pltpu.CompilerParams(collective_id=2, has_side_effects=True, vmem_limit_bytes=62 * MIB)
    else:
        out_shape += (
            jax.ShapeDtypeStruct((2 * D // LANES, LANES), f32),
            jax.ShapeDtypeStruct((2, 2, TILES, QKV_ROWS, LANES), bf16),
        )
        out_specs += (vmem, hbm)
        scratch += [VMEM((6, TILES, TILE, 3 * D), bf16), dma((2 * OUT_AT,))]
        params = pltpu.CompilerParams(vmem_limit_bytes=60 * MIB)
    return pl.pallas_call(
        functools.partial(rear_kernel, comm, per, seq),
        out_shape=out_shape,
        in_specs=in_specs,
        out_specs=out_specs,
        scratch_shapes=scratch,
        compiler_params=params,
        name="rear",
    )(*args)


def step_kernel(per, g_hbm, *refs):
    ins, outs, bufs, done = refs[:5], refs[5:9], refs[9:14], refs[14:18]
    g_buf, in_sems, out_sems = refs[18:]

    def loads(s):
        yield pltpu.make_async_copy(g_hbm.at[s], g_buf.at[s], in_sems.at[6 * s])
        for n in range(5):
            yield pltpu.make_async_copy(ins[n].at[s], bufs[n].at[s], in_sems.at[6 * s + 1 + n])

    def stores(s):
        for n in range(4):
            yield pltpu.make_async_copy(done[n].at[s], outs[n].at[s], out_sems.at[4 * s + n])

    for s in range(per):
        for c in loads(s):
            c.start()
    w, ls, rs, lr, rr = bufs
    grad, new_l, new_r, new_w = done
    for first in range(0, per, 2):
        group = range(first, min(first + 2, per))
        for s in group:
            for c in loads(s):
                c.wait()
        for s in group:
            low = g_buf[s]
            grad[s] = low.astype(f32)
            inner = dot(low, rr[s].astype(bf16)).astype(bf16)
            new_l[s] = 0.5 * ls[s] + 0.5 * dot_nt(low, low)
            new_r[s] = 0.5 * rs[s] + 0.5 * dot_tn(low, low)
            new_w[s] = w[s] - dot(lr[s].astype(bf16), inner)
        for s in group:
            for c in stores(s):
                c.start()
    for s in range(per):
        for c in stores(s):
            c.wait()


def owner_step(owned, weights, ls, rs, lr, rr):
    per = weights.shape[0]
    any_spec = pl.BlockSpec(memory_space=pl.ANY)
    dma = pltpu.SemaphoreType.DMA
    return pl.pallas_call(
        functools.partial(step_kernel, per),
        out_shape=(jax.ShapeDtypeStruct(weights.shape, f32),) * 4,
        in_specs=[any_spec] * 6,
        out_specs=(any_spec,) * 4,
        scratch_shapes=[VMEM(weights.shape, f32)] * 9
        + [VMEM(weights.shape, bf16), dma((6 * per,)), dma((4 * per,))],
        compiler_params=pltpu.CompilerParams(vmem_limit_bytes=60 * MIB),
        name="owner_step",
    )(owned, weights, ls, rs, lr, rr)


def pack_tail(vec, devices):
    half = vec.shape[0] // (2 * devices)
    wide = jnp.pad(vec.reshape(devices, 2, half), ((0, 0), (0, 0), (0, TAIL * BLK - half)))
    return wide.reshape(devices, 2, TAIL, BLK)


def unpack_tail(tails, half):
    lead = tails.shape[:-2]
    return tails.reshape(lead + (TAIL * BLK,))[..., :half].reshape(-1)


def from_rows(rows):
    cut = rows.reshape(2, 16, -1, TILE, LANES).transpose(2, 1, 3, 0, 4)
    return cut.reshape(-1, BLK, BLK)


def sum_places():
    def place(b):
        row, part, group = b // 9, (b % 9) // 3, b % 3
        return b - OUT_AT if b >= OUT_AT else ALL - OUT_AT + 9 * group + 3 * row + part

    return [place(b) for b in range(ALL)]


def shards(
    inputs, cotangent, lengths, owner_slot, weights, vectors,
    left_stat, right_stat, left_root, right_root, vector_stat,
):
    per, size = weights.shape[0], vectors.shape[0]
    chips = lax.axis_size("fsdp")
    chip, core = lax.axis_index("fsdp"), lax.axis_index("dp")
    comm = chips == 16
    rows = per * HALF
    slots = jnp.arange(chips * per, dtype=jnp.int32)
    tail = pack_tail(vectors.astype(bf16), 1)[0]
    if comm:
        role = slots // per
        turned = (role // 4) * 4 + (role % 2) * 2 + (role // 2) % 2
        by_role = jnp.where(core == 0, slots, turned * per + slots % per)
        numbers = jnp.asarray(sum_places(), jnp.int32) + 1
        inverse = jnp.sum(jnp.where(by_role[:, None] == owner_slot[None, :], numbers[None, :], 0), axis=1) - 1
        w_all = gather(weights, tail)
    else:
        low = weights.astype(bf16).reshape(per, 2, HALF, BLK).transpose(1, 0, 2, 3).reshape(2, rows, BLK)
        w_all = lax.all_gather(jnp.concatenate([low, tail], axis=1), "fsdp", axis=0)
    vec = unpack_tail(w_all[:, :, rows:, :], size // 2).astype(f32)[None, :]
    w_all = w_all.reshape(chips, 2, -1, TILE, BLK)
    qkv, mixed, lse, wq = front(owner_slot, lengths, inputs, w_all, vec, per)
    outputs, d_one, d_mixed, vg_rest, g_rest = middle(
        owner_slot, lengths, inputs, cotangent, mixed, vec, w_all, per)
    if comm:
        input_grad, vec_sum, owned = rear(
            lengths, inputs, qkv, d_mixed, lse, d_one, wq, g_rest, vg_rest, inverse, per)
    else:
        input_grad, vg_qv, g_qkv = rear(lengths, inputs, qkv, d_mixed, lse, d_one, wq)
        vec_sum = lax.psum(jnp.concatenate([vg_qv, vg_rest], axis=0), ("dp", "fsdp"))
        blocks = from_rows(jnp.concatenate([g_qkv, g_rest], axis=3)).astype(f32)
        by_slot = jnp.zeros((chips * per, BLK, BLK), f32).at[owner_slot].set(blocks)
        owned = lax.psum(lax.psum_scatter(by_slot, "fsdp", scatter_dimension=0, tiled=True), "dp").astype(bf16)
    grad, new_left, new_right, new_weights = owner_step(
        owned, weights, left_stat, right_stat, left_root, right_root)
    vec_grad = lax.dynamic_slice(vec_sum.reshape(-1), (chip * size,), (size,))
    new_stat = 0.5 * vector_stat + 0.5 * vec_grad * vec_grad
    new_vectors = vectors - 0.1 * vec_grad * lax.rsqrt(new_stat + VEC_EPS)
    return (outputs, input_grad, grad, new_left, new_right, new_weights, vec_grad, new_stat, new_vectors)


def solution(mesh):
    tokens = P(("dp", "fsdp"), None)
    blocks, packed = P("fsdp", None, None), P("fsdp")
    return jax.shard_map(
        shards,
        mesh=mesh,
        in_specs=(tokens, tokens, P(("dp", "fsdp")), P(), blocks, packed, blocks, blocks, blocks, blocks, packed),
        out_specs=(tokens, tokens, blocks, blocks, blocks, blocks, packed, packed, packed),
        check_vma=False,
    )
```

```python
import functools
import math

import jax
import jax.numpy as jnp
from jax import lax
from jax.experimental import pallas as pl
from jax.experimental.pallas import tpu as pltpu
from jax.sharding import PartitionSpec as P

D = 768
HEADS = 12
HEAD = 64
FF = 3072
BLK = 256
HALF = BLK // 2
TAIL = 16
LANES = 128
TILE = 16
TILES = HALF // TILE
LN_EPS = 1e-06
FILL = -1000000000.0
VEC_EPS = 1e-12
SCALE = HEAD ** (-0.5)
MIB = 1024 * 1024
WIDE = 1024

f32 = jnp.float32
bf16 = jnp.bfloat16
MESH = pl.DeviceIdType.MESH
VMEM = pltpu.VMEM
SMEM = pltpu.SMEM

QKV_AT, OUT_AT, UP_AT, DOWN_AT, ALL = 0, 27, 36, 72, 108
REST_ROWS, QKV_ROWS = (ALL - OUT_AT) * TILE, OUT_AT * TILE
GROUP_ROWS = QKV_ROWS // 3

B_Q, B_V, B_O, G_ONE, S_ONE, B_UP, B_DOWN, G_TWO, S_TWO = (
    0, 768, 1536, 2304, 3072, 3840, 6912, 7680, 8448)

LATE_Z = (False, False, True, True, True, True)
STEPS = (
    (),
    (),
    (),
    ("0b2",),
    ("0b6", "1b3",),
    ("0b4", "0b3", "1b5",),
    ("2b0",),
    ("0b0", "0z3", "1b2", "0b5", "1z3",),
    ("1b4", "0z0",),
    ("2a0", "1z2", "1b1",),
    ("2b3", "2b4", "2b6", "1b0", "3b3", "3b2", "0z2", "3b5", "2b1",),
    ("1z1", "4b3", "2a3", "1w1",),
    ("1b6", "4b1", "3b0", "1w0", "2b5", "4b0",),
    ("1z0", "0b7",),
    ("0w0", "3b1", "2a1", "0b1", "0w1",),
    ("4b5", "4b2", "2z0", "4a1", "3a0", "2z1", "3b4", "2b2", "1a0",),
    ("3a1", "5b1", "0z1", "5b3", "4a0", "5b0", "v0", "5b4", "4b4", "5b2", "4a2",),
    ("v1", "5b5", "5a1", "4z1", "2a2", "4b6", "3z0", "3z1", "0a0", "1b7", "v2", "5a0", "3a2", "4z0", "3b6",
     "5a2", "5z1", "5b6", "2w0", "4w0", "3a3",),
    ("v3", "5b7", "2b7", "5a3", "3b7", "5z0", "5w0", "4b7", "4a3", "3w0", "0f", "2f", "1f", "v4", "5f", "4f",
     "3f", "v5",),
)


def dot(a, b):
    return lax.dot_general(a, b, (((1,), (0,)), ((), ())), preferred_element_type=f32)


def dot_nt(a, b):
    return lax.dot_general(a, b, (((1,), (1,)), ((), ())), preferred_element_type=f32)


def dot_tn(a, b):
    return lax.dot_general(a, b, (((0,), (0,)), ((), ())), preferred_element_type=f32)


def cols(index, width):
    return pl.ds(pl.multiple_of(index * width, width), width)


def fetch(slot_ref, w_hbm, buf, sem, block, row, col, start):
    at = pl.multiple_of(slot_ref[block] * TILES, TILES) if start else 0
    return pltpu.make_async_copy(
        w_hbm.at[:, pl.ds(at, TILES), :, :], buf.at[pl.ds(2 * row, 2), :, :, cols(col, BLK)], sem)


def put(buf, g_hbm, sems, n, row, col):
    for half in range(2):
        yield pltpu.make_async_copy(
            buf.at[pl.ds(2 * row, 2), :, :, pl.ds(col * BLK + half * LANES, LANES)],
            g_hbm.at[half, :, :, pl.ds(n * TILE, TILE), :],
            sems.at[2 * n + half],
        )


def panel(buf, col, width):
    got = buf[:, :, :, cols(col, width)]
    return got.reshape(got.shape[0] * HALF, width)


def front_kernel(seq, slot, lens, x_hbm, w_hbm, vec, qkv_out, mixed_out, lse_out, wq_out, x, qkv, mixed, lse, wbuf, even, odd, sems, io_sems):
    def in_part(part, start):
        for row in range(3):
            for col in range(3 * part, 3 * part + 3):
                block = row * 9 + col
                yield fetch(slot, w_hbm, wbuf, sems.at[block], QKV_AT + block, row, col, start)

    load_x = pltpu.make_async_copy(x_hbm, x, io_sems.at[0])
    load_x.start()
    for part in range(3):
        for c in in_part(part, True):
            c.start()
    load_x.wait()
    saves = []
    for part in range(3):
        for c in in_part(part, False):
            c.wait()
        at = slice(part * D, (part + 1) * D)
        got = dot(x[...], wbuf[:, :, :, at].reshape(D, D))
        if part != 1:
            bias = B_Q if part == 0 else B_V
            got = got + vec[:, bias:bias + D]
        qkv[:, at] = got.astype(bf16)
        saves.append(pltpu.make_async_copy(qkv.at[:, at], qkv_out.at[:, at], io_sems.at[1 + part]))
        saves[-1].start()
    saves.append(pltpu.make_async_copy(wbuf, wq_out, io_sems.at[8]))
    saves[-1].start()

    lane = lax.broadcasted_iota(jnp.int32, (seq, 2 * HEAD), 1)
    key = lax.broadcasted_iota(jnp.int32, (1, seq), 1)

    def where(item):
        sent, pair = item // 6, item % 6
        return sent, pair, pl.ds(pl.multiple_of(sent * seq, seq), seq)

    def score(item, buf):
        sent, pair, rows = where(item)
        q = qkv[rows, cols(pair, 128)] * SCALE
        k = qkv[rows, cols(6 + pair, 128)]
        two = jnp.concatenate([jnp.where(lane < HEAD, q, 0), jnp.where(lane >= HEAD, q, 0)], axis=0)
        buf[...] = dot_nt(two, k)

    def attend(item, buf):
        sent, pair, rows = where(item)
        v = qkv[rows, cols(12 + pair, 128)]
        scores = jnp.where(key < lens[sent], buf[...], FILL)
        top = jnp.max(scores, axis=-1, keepdims=True)
        expo = jnp.exp(scores - top).astype(bf16)
        values = [
            jnp.concatenate([jnp.where((lane < HEAD) == (h == 0), v, 0), jnp.where(lane == h, 1, 0).astype(bf16)], axis=1)
            for h in range(2)
        ]
        got = dot(jnp.concatenate([expo[:seq], expo[seq:]], axis=1), jnp.concatenate(values, axis=0))
        sums = got[:, 128:130]
        inverse = 1.0 / sums
        mixed[rows, cols(pair, 128)] = (
            got[:, :128] * jnp.where(lane < HEAD, inverse[:, 0:1], inverse[:, 1:2])).astype(bf16)
        logs = jnp.log(sums)
        kept = jnp.where(lane == 2 * pair, top[:seq] + logs[:, 0:1], lse[rows, :])
        lse[rows, :] = jnp.where(lane == 2 * pair + 1, top[seq:] + logs[:, 1:2], kept)

    def both(i, carry):
        score(2 * i + 1, odd)
        attend(2 * i, even)
        score(jnp.minimum(2 * i + 2, 11), even)
        attend(2 * i + 1, odd)
        return carry

    lse[...] = jnp.zeros_like(lse)
    score(0, even)
    for sent in range(x.shape[0] // seq):
        lax.fori_loop(3 * sent, 3 * sent + 3, both, 0)
        rows = pl.ds(sent * seq, seq)
        for n, (src, dst) in enumerate(((mixed, mixed_out), (lse, lse_out))):
            saves.append(pltpu.make_async_copy(src.at[rows, :], dst.at[rows, :], io_sems.at[4 + 2 * sent + n]))
            saves[-1].start()
    for c in saves:
        c.wait()


def front(slot, lens, x, w_all, vec):
    tok = x.shape[0]
    seq = tok // lens.shape[0]
    any_spec = pl.BlockSpec(memory_space=pl.ANY)
    smem, vmem = pl.BlockSpec(memory_space=SMEM), pl.BlockSpec(memory_space=VMEM)
    return pl.pallas_call(
        functools.partial(front_kernel, seq),
        out_shape=(
            jax.ShapeDtypeStruct((tok, 3 * D), bf16),
            jax.ShapeDtypeStruct((tok, D), bf16),
            jax.ShapeDtypeStruct((tok, 128), f32),
            jax.ShapeDtypeStruct((6, TILES, TILE, 3 * D), bf16),
        ),
        in_specs=[smem, smem, any_spec, any_spec, vmem],
        out_specs=(any_spec,) * 4,
        scratch_shapes=[
            VMEM((tok, D), bf16), VMEM((tok, 3 * D), bf16), VMEM((tok, D), bf16), VMEM((tok, 128), f32),
            VMEM((6, TILES, TILE, 3 * D), bf16), VMEM((2 * seq, seq), f32), VMEM((2 * seq, seq), f32),
            pltpu.SemaphoreType.DMA((27,)), pltpu.SemaphoreType.DMA((9,)),
        ],
        compiler_params=pltpu.CompilerParams(vmem_limit_bytes=60 * MIB),
        name="front",
    )(slot, lens, x, w_all, vec)


def norm(hidden):
    center = hidden - jnp.mean(hidden, axis=-1, keepdims=True)
    spread = jnp.mean(center * center, axis=-1, keepdims=True)
    rstd = lax.rsqrt(spread + LN_EPS)
    return center * rstd, rstd


def norm_back(grad, normed, rstd, gain):
    scaled = grad * gain
    return rstd * (
        scaled
        - jnp.mean(scaled, axis=-1, keepdims=True)
        - normed * jnp.mean(scaled * normed, axis=-1, keepdims=True)
    )


def col_sum(a):
    return jnp.sum(a, axis=0, keepdims=True)


def gelu_and_slope(z):
    cdf = 0.5 + 0.5 * lax.erf(z * math.sqrt(0.5))
    density = jnp.exp2(z * z * (-0.5 / math.log(2.0))) * (1.0 / math.sqrt(2.0 * math.pi))
    return z * cdf, cdf + z * density


def middle_kernel(
    seq, slot, lens, x_hbm, cot_hbm, mixed_hbm, vec, w_hbm,
    outputs_hbm, d_one_hbm, d_mixed_hbm, vgrad, g_hbm,
    x, cot, mixed, outputs, d_one_out, d_mixed,
    w_out, w_up, w_down, act, y_low, dz_up, dz_down, slope, h_buf, n_buf, sems, put_sems, in_sems, out_sems,
):
    tok = x.shape[0]
    places = (
        [(OUT_AT + i, w_out, i // 3, i % 3) for i in range(9)]
        + [(UP_AT + i, w_up, i // 12, i % 12) for i in range(36)]
        + [(DOWN_AT + i, w_down, i // 3, i % 3) for i in range(36)]
    )

    def copies(kind, lo, hi):
        for block, buf, row, col in places:
            if lo <= block < hi:
                if kind != "put":
                    yield fetch(slot, w_hbm, buf, sems.at[block - OUT_AT], block, row, col, kind == "get")
                else:
                    yield from put(buf, g_hbm, put_sems, block - OUT_AT, row, col)

    def first(sent, lo, hi):
        @pl.when(sent == 0)
        def _():
            for c in copies("got", lo, hi):
                c.wait()

    loads = [
        pltpu.make_async_copy(src, dst, in_sems.at[n])
        for n, (src, dst) in enumerate(((mixed_hbm, mixed), (x_hbm, x), (cot_hbm, cot)))
    ]
    loads[0].start()
    for c in copies("get", OUT_AT, UP_AT):
        c.start()
    loads[1].start()
    for c in copies("get", UP_AT, 108):
        c.start()
    loads[2].start()

    def save(n, src, dst, sent):
        rows = pl.ds(pl.multiple_of(sent * seq, seq), seq)
        return pltpu.make_async_copy(src.at[rows, :], dst.at[rows, :], out_sems.at[n, sent])

    def vec_at(at, width=D):
        return vec[:, at:at + width]

    def vadd(at, value):
        for t in range(value.shape[1] // LANES):
            row = (at - B_O) // LANES + t
            vgrad[row:row + 1, :] += value[:, t * LANES:(t + 1) * LANES]

    vgrad[...] = jnp.zeros_like(vgrad)

    def tile(sent, carry):
        rows = pl.ds(pl.multiple_of(sent * seq, seq), seq)
        first(sent, OUT_AT, UP_AT)

        @pl.when(sent == 0)
        def _():
            loads[0].wait()
            loads[1].wait()

        att = dot(mixed[rows, :], w_out[...].reshape(D, D)) + vec_at(B_O)
        n_one, r_one = norm(x[rows, :].astype(f32) + att)
        n_buf[...] = n_one
        y_one = n_one * vec_at(G_ONE) + vec_at(S_ONE)
        h_buf[...] = y_one
        y_low[rows, :] = y_one.astype(bf16)
        first(sent, UP_AT, DOWN_AT)

        for j in range(FF // WIDE):
            at = slice(j * WIDE, (j + 1) * WIDE)
            z = dot(y_low[rows, :], panel(w_up, j, WIDE)) + vec_at(B_UP + j * WIDE, WIDE)
            got, got_slope = gelu_and_slope(z)
            act[rows, at] = got.astype(bf16)
            slope[:, at] = got_slope
        first(sent, DOWN_AT, 108)

        @pl.when(sent == 0)
        def _():
            loads[2].wait()


        z_down = dot(act[rows, :], w_down[...].reshape(FF, D)) + vec_at(B_DOWN)
        n_two, r_two = norm(h_buf[...] + z_down)
        outputs[rows, :] = (n_two * vec_at(G_TWO) + vec_at(S_TWO)).astype(bf16)
        save(0, outputs, outputs_hbm, sent).start()

        live = lax.broadcasted_iota(jnp.int32, (seq, 1), 0) < lens[sent]
        grad = jnp.where(live, cot[rows, :].astype(f32), 0.0)
        vadd(G_TWO, col_sum(grad * n_two))
        vadd(S_TWO, col_sum(grad))
        d_two = norm_back(grad, n_two, r_two, vec_at(G_TWO))
        h_buf[...] = d_two
        low = d_two.astype(bf16)
        dz_down[rows, :] = low
        vadd(B_DOWN, col_sum(low.astype(f32)))

        for j in range(FF // WIDE):
            at = slice(j * WIDE, (j + 1) * WIDE)
            w = w_down[j * WIDE // HALF:(j + 1) * WIDE // HALF, :, :].reshape(WIDE, D)
            got = (dot_nt(dz_down[rows, :], w) * slope[:, at]).astype(bf16)
            dz_up[rows, at] = got
            vadd(B_UP + j * WIDE, col_sum(got.astype(f32)))

        d_y = h_buf[...] + dot_nt(dz_up[rows, :], w_up[...].reshape(D, FF))
        vadd(G_ONE, col_sum(d_y * n_buf[...]))
        vadd(S_ONE, col_sum(d_y))
        d_one = norm_back(d_y, n_buf[...], r_one, vec_at(G_ONE))
        d_one_out[rows, :] = d_one
        d_low = d_one.astype(bf16)
        vadd(B_O, col_sum(d_low.astype(f32)))
        d_mixed[rows, :] = dot_nt(d_low, w_out[...].reshape(D, D)).astype(bf16)
        save(1, d_one_out, d_one_hbm, sent).start()
        save(2, d_mixed, d_mixed_hbm, sent).start()
        return carry

    lax.fori_loop(0, tok // seq, tile, 0)

    for i in range(FF // WIDE):
        got = dot_tn(act[:, i * WIDE:(i + 1) * WIDE], dz_down[...])
        w_down[i * WIDE // HALF:(i + 1) * WIDE // HALF, :, :] = got.astype(bf16).reshape(WIDE // HALF, TILES, TILE, D)
        for c in copies("put", DOWN_AT + 12 * i, DOWN_AT + 12 * (i + 1)):
            c.start()
    for i in range(FF // WIDE):
        got = dot_tn(y_low[...], dz_up[:, i * WIDE:(i + 1) * WIDE])
        w_up[:, :, :, i * WIDE:(i + 1) * WIDE] = got.astype(bf16).reshape(6, TILES, TILE, WIDE)
        for row in range(3):
            for c in copies("put", UP_AT + 12 * row + 4 * i, UP_AT + 12 * row + 4 * (i + 1)):
                c.start()
    w_out[...] = dot_tn(mixed[...], d_one_out[...].astype(bf16)).astype(bf16).reshape(6, TILES, TILE, D)
    for c in copies("put", OUT_AT, UP_AT):
        c.start()
    for sent in range(tok // seq):
        save(0, outputs, outputs_hbm, sent).wait()
        save(1, d_one_out, d_one_hbm, sent).wait()
        save(2, d_mixed, d_mixed_hbm, sent).wait()
    for c in copies("put", OUT_AT, 108):
        c.wait()


def middle(slot, lens, x, cot, mixed, vec, w_all):
    tok = x.shape[0]
    seq = tok // lens.shape[0]
    any_spec = pl.BlockSpec(memory_space=pltpu.HBM)
    smem, vmem = pl.BlockSpec(memory_space=SMEM), pl.BlockSpec(memory_space=VMEM)
    return pl.pallas_call(
        functools.partial(middle_kernel, seq),
        out_shape=(
            jax.ShapeDtypeStruct((tok, D), bf16),
            jax.ShapeDtypeStruct((tok, D), f32),
            jax.ShapeDtypeStruct((tok, D), bf16),
            jax.ShapeDtypeStruct(((vec.shape[1] - B_O) // LANES, LANES), f32),
            jax.ShapeDtypeStruct((2, 2, TILES, REST_ROWS, LANES), bf16),
        ),
        in_specs=[smem, smem, any_spec, any_spec, any_spec, vmem, any_spec],
        out_specs=(any_spec, any_spec, any_spec, vmem, any_spec),
        scratch_shapes=[
            VMEM((tok, D), bf16),
            VMEM((tok, D), bf16),
            VMEM((tok, D), bf16),
            VMEM((tok, D), bf16),
            VMEM((tok, D), f32),
            VMEM((tok, D), bf16),
            VMEM((6, TILES, TILE, D), bf16),
            VMEM((6, TILES, TILE, FF), bf16),
            VMEM((24, TILES, TILE, D), bf16),
            VMEM((tok, FF), bf16),
            VMEM((tok, D), bf16),
            VMEM((tok, FF), bf16),
            VMEM((tok, D), bf16),
            VMEM((seq, FF), f32),
            VMEM((seq, D), f32),
            VMEM((seq, D), f32),
            pltpu.SemaphoreType.DMA((81,)),
            pltpu.SemaphoreType.DMA((162,)),
            pltpu.SemaphoreType.DMA((3,)),
            pltpu.SemaphoreType.DMA((3, tok // seq)),
        ],
        compiler_params=pltpu.CompilerParams(vmem_limit_bytes=63 * MIB),
        name="middle",
    )(slot, lens, x, cot, mixed, vec, w_all)


class Place:
    def __init__(self):
        chip = lax.axis_index("fsdp")
        self.core, self.me = lax.axis_index("dp"), chip
        z, y, x = chip // 4, (chip // 2) % 2, chip % 2
        core = self.core
        self.z, self.a, self.b = z, y * (1 - core) + x * core, x * (1 - core) + y * core
        self.near, self.mid, self.far = z + 1 - 2 * (z % 2), (z + 2) % 4, 3 - z
        self.index = z * 4 + self.a * 2 + self.b
        self.peer_a = core, self.chip(z, 1 - self.a, self.b)
        self.peer_b = core, self.chip(z, self.a, 1 - self.b)
        self.peer_z = core, self.chip(self.near, self.a, self.b)
        self.peer_w = core, self.chip(self.far, self.a, self.b)
        self.sibling = 1 - core, chip

    def chip(self, z, a, b):
        return z * 4 + a * (2 - self.core) + b * (1 + self.core)

    def at_index(self, index):
        return self.core, self.chip(index // 4, (index // 2) % 2, index % 2)

    def others(self):
        return [self.at_index((self.index + k) % 16) for k in range(1, 16)]

    def near_peers(self):
        return [self.peer_a, self.peer_b, self.peer_z, self.peer_w]

    def greet(self, peers, meanwhile=lambda: None):
        barrier = pltpu.get_barrier_semaphore()
        peers = peers + [self.sibling]
        for peer in peers:
            pl.semaphore_signal(barrier, inc=1, device_id=peer, device_id_type=MESH)
        meanwhile()
        pl.semaphore_wait(barrier, len(peers))


def remote(src, dst, send_sem, recv_sem, to):
    return pltpu.make_async_remote_copy(
        src_ref=src, dst_ref=dst, send_sem=send_sem, recv_sem=recv_sem, device_id=to, device_id_type=MESH)


def chunk_rows(total, parts, tile=16):
    tiles, first, got = total // tile, 0, []
    for i in range(parts):
        rows = (tiles // parts + (i < tiles % parts)) * tile
        got.append((first, rows))
        first += rows
    return got


def in_turns(lags, parts):
    for turn in range(parts + lags[-1]):
        for n, lag in enumerate(lags):
            if 0 <= turn - lag < parts:
                yield n, turn - lag


def gather_kernel(chunks, w, tail, out, tails, own, keep_sem, send_sems, main_sems, sib_sems, tail_out, tail_in):
    p = Place()

    def cast():
        for i in range(w.shape[0]):
            own[:, i * HALF:(i + 1) * HALF, :] = w[i].astype(bf16).reshape(2, HALF, BLK)

    p.greet(p.others(), cast)
    keep = pltpu.make_async_copy(own, out.at[:, p.me], keep_sem)

    def tail_copy(k, back):
        to = p.at_index((p.index + k) % 16)
        chip = to[1] if back else p.me
        return remote(tail, tails.at[chip], tail_out.at[k], tail_in.at[chip], to)

    sends = []
    a, b = p.a, p.b

    def window(i):
        return pl.ds(*chunks[i])

    def send(i, chip, *peers):
        src = own.at[p.core, window(i), :] if chip is p.me else out.at[p.core, chip, window(i), :]
        for to in peers:
            sems = sib_sems if to is p.sibling else main_sems
            c = pltpu.make_async_remote_copy(
                src_ref=src, dst_ref=out.at[p.core, chip, window(i), :],
                send_sem=send_sems.at[len(sends)], recv_sem=sems.at[i, chip], device_id=to, device_id_type=MESH)
            c.start()
            sends.append(c)

    def arrive(i, chip, half, sems):
        there = out.at[half, chip, window(i), :]
        pltpu.make_async_remote_copy(
            src_ref=there, dst_ref=there, send_sem=send_sems.at[0], recv_sem=sems.at[i, chip],
            device_id=p.sibling, device_id_type=MESH).wait_recv()

    def forward(i, chip, *peers):
        arrive(i, chip, p.core, main_sems)
        send(i, chip, *peers, p.sibling)

    def stage(n, i):
        z_first = i == 0
        if n == 0 and z_first:
            forward(i, p.chip(p.far, a, b), p.peer_z, p.peer_a, p.peer_b)
        elif n == 1 and z_first:
            for zz in (p.near, p.mid):
                forward(i, p.chip(zz, a, b), p.peer_a, p.peer_b)
        elif n == 2 and z_first:
            for zz in (p.z, p.far, p.near, p.mid):
                forward(i, p.chip(zz, 1 - a, b), p.peer_b)
        elif n == 0:
            forward(i, p.chip(p.z, 1 - a, b), p.peer_w, p.peer_z, p.peer_b)
        elif n == 1:
            for aa in (a, 1 - a):
                forward(i, p.chip(p.far, aa, b), p.peer_z, p.peer_b)
        elif n == 2:
            for zz in (p.near, p.mid):
                for aa in (a, 1 - a):
                    forward(i, p.chip(zz, aa, b), p.peer_b)
        else:
            for zz in (p.z, p.far, p.near, p.mid):
                for aa in (a, 1 - a):
                    forward(i, p.chip(zz, aa, 1 - b))

    for i in range(len(chunks)):
        if i == 0:
            send(i, p.me, p.peer_w, p.peer_z, p.peer_a, p.peer_b)
        else:
            send(i, p.me, p.peer_a, p.peer_w, p.peer_z, p.peer_b)
    keep.start()
    for k in range(1, 16):
        tail_copy(k, False).start()
    tails[p.me] = tail[...]
    for n, i in in_turns((0, 2, 3, 4), len(chunks)):
        stage(n, i)
    for i in range(len(chunks)):
        for k in range(1, 16):
            arrive(i, (p.me + k) % 16, 1 - p.core, sib_sems)
    for k in range(1, 16):
        tail_copy(k, True).wait_recv()
    for c in sends:
        c.wait_send()
    for k in range(1, 16):
        tail_copy(k, False).wait_send()
    keep.wait()


def gather(weights, tail):
    shape = (2, weights.shape[0] * HALF, BLK)
    chunks = chunk_rows(shape[1], 3)
    vmem = pl.BlockSpec(memory_space=VMEM)
    dma = pltpu.SemaphoreType.DMA
    return pl.pallas_call(
        functools.partial(gather_kernel, chunks),
        out_shape=(
            jax.ShapeDtypeStruct((2, 16) + shape[1:], bf16), jax.ShapeDtypeStruct((16, TAIL, LANES), bf16)),
        in_specs=[vmem, vmem],
        out_specs=(pl.BlockSpec(memory_space=pl.ANY), vmem),
        scratch_shapes=[
            VMEM(shape, bf16), dma, dma((30 * len(chunks),)), dma((len(chunks), 16)), dma((len(chunks), 16)),
            dma((16,)), dma((16,)),
        ],
        compiler_params=pltpu.CompilerParams(
            collective_id=1, has_side_effects=True, vmem_limit_bytes=60 * MIB),
        name="gather",
    )(weights, tail)


class Sums:
    def __init__(self, place, chunks, late_z, ready, mine, sib, got_b, got_a, got_z, got_w, result, send_sems, recv_sems):
        self.p, self.chunks, self.late_z, self.ready = place, chunks, late_z, ready
        self.mine, self.sib, self.result = mine, sib, result
        self.got = {"b": got_b, "a": got_a, "z": got_z, "w": got_w}
        self.send_sems, self.recv_sems = send_sems, recv_sems
        self.begun = set()

    def shard(self, i, name):
        p, k = self.p, int(name[1:] or 0)
        zs, sides = (p.near, p.mid, p.far, p.z), (1 - p.a, p.a)
        if self.late_z[i]:
            order = [(z, a) for a in sides for z in zs]
            first = {"b": 0, "a": 0, "z": 4, "w": 6, "f": 7}[name[0]]
        else:
            order = [(z, a) for z in zs for a in sides]
            first = {"b": 0, "z": 0, "w": 4, "a": 6, "f": 7}[name[0]]
        return (*order[first + k], 1 - p.b if name[0] == "b" else p.b)

    def parts(self, i, name):
        k = int(name[1:] or 0)
        if self.late_z[i]:
            return {
                "b": (), "a": (f"b{k}",), "z": (f"b{4 + k}", f"a{k}"), "w": ("b6", "a2", "z1"),
                "f": ("b7", "a3", "z0", "w0")}[name[0]]
        return {
            "b": (), "z": (f"b{k}",), "w": (f"b{4 + k}", f"z{2 + k}"), "a": ("b6", "z0", "w0"),
            "f": ("b7", "z1", "w1", "a0")}[name[0]]

    def names(self, i):
        rest = ("a0", "a1", "a2", "a3", "z0", "z1", "w0") if self.late_z[i] else ("z0", "z1", "z2", "z3", "w0", "w1", "a0")
        return [f"b{k}" for k in range(8)] + list(rest)

    def copy(self, i, name):
        p = self.p
        at = pl.ds(*self.chunks[i])
        to = {"b": p.peer_b, "a": p.peer_a, "z": p.peer_z, "w": p.peer_w}[name[0]]
        n = self.names(i).index(name)
        return remote(
            self.mine.at[(*self.shard(i, name), at, slice(None))],
            self.got[name[0]].at[int(name[1:]), at, :],
            self.send_sems.at[i, n], self.recv_sems.at[i, n], to)

    def step(self, i, name):
        if i not in self.begun:
            self.begun.add(i)
            self.ready(i)
        parts = self.parts(i, name)
        for part in parts:
            self.copy(i, part).wait_recv()
        where = self.shard(i, name)
        lo, number = self.chunks[i]

        def add(n, carry):
            at = pl.ds(pl.multiple_of(lo + n * GROUP_ROWS, TILE), GROUP_ROWS)
            here = (*where, at, slice(None))
            if not parts:
                self.mine[here] = self.mine[here] + self.sib[here]
                return carry
            acc = self.mine[here].astype(f32) + self.sib[here].astype(f32)
            for part in parts:
                acc = acc + self.got[part[0]][int(part[1:]), at, :].astype(f32)
            low = acc.astype(bf16)
            if name == "f":
                blocks = GROUP_ROWS // TILE
                self.result[pl.ds(lo // TILE + n * blocks, blocks), :, :] = low.reshape(blocks, TILE, LANES)
            else:
                self.mine[here] = low
            return carry

        lax.fori_loop(0, number // GROUP_ROWS, add, 0)
        if name != "f":
            self.copy(i, name).start()

    def end(self):
        for i in range(len(self.chunks)):
            for name in self.names(i):
                self.copy(i, name).wait_send()


def rear_kernel(comm, per, seq, lens, x_hbm, qkv_hbm, d_mixed_hbm, lse, d_one_hbm, wq, *refs):
    tok = x_hbm.shape[0]
    if comm:
        (
            g_rest, vg_rest, inverse, input_grad_hbm, vec_sum, owned,
            x, qkv, d_mixed, d_one, input_grad, wbuf, d_qkv, lse_t, in_sems, out_sems,
            mine, sib, got_b, got_a, got_z, got_w, give, result, picked, g_own, g_sib, vec_got,
            keep_sems, sib_send, sib_recv, rs_send, rs_recv, xs_send, xs_recv, pair_sems, vec_send, vec_recv,
        ) = refs
        p = Place()
        p.greet(p.others())
        chunks = [(i * QKV_ROWS, QKV_ROWS) for i in range(3)] + [(REST_ROWS + g * GROUP_ROWS, GROUP_ROWS) for g in range(3)]

        def sib_copy(i):
            at = pl.ds(*chunks[i])
            if i < 3:
                src = g_rest.at[1 - p.core, :, :, :, at, :]
            else:
                src = give.at[:, :, :, pl.ds((i - 3) * GROUP_ROWS, GROUP_ROWS), :]
            return remote(src, sib.at[:, :, :, at, :], sib_send.at[i], sib_recv.at[i], p.sibling)

        def keep(i):
            at = pl.ds(*chunks[i])
            return pltpu.make_async_copy(g_rest.at[p.core, :, :, :, at, :], mine.at[:, :, :, at, :], keep_sems.at[i])

        def ready(i):
            if i < 3:
                keep(i).wait()
            sib_copy(i).wait_recv()

        for i in range(3):
            sib_copy(i).start()
            keep(i).start()
        sums = Sums(
            p, chunks, LATE_Z, ready, mine, sib, got_b, got_a, got_z, got_w, result, rs_send, rs_recv)
        chip = lax.axis_index("fsdp")
        z, y, x_at = chip // 4, (chip // 2) % 2, chip % 2
        hops = (
            p.sibling, (p.core, z * 4 + y * 2 + 1 - x_at), (p.core, z * 4 + (1 - y) * 2 + x_at), p.peer_z, p.peer_w)

        def vec_copy(n):
            return remote(vec_got.at[2 * n], vec_got.at[2 * n + 1], vec_send.at[n], vec_recv.at[n], hops[n])

        def vec_step(n):
            if n > 0:
                vec_copy(n - 1).wait_recv()
                vec_sum[...] = vec_sum[...] + vec_got[2 * n - 1]
            if n < 5:
                vec_got[2 * n] = vec_sum[...]
                vec_copy(n).start()

        def after(step):
            for name in STEPS[step + 1]:
                if name[0] == "v":
                    vec_step(int(name[1:]))
                else:
                    sums.step(int(name[0]), name[1:])
    else:
        (
            input_grad_hbm, vec_sum, g_qkv,
            x, qkv, d_mixed, d_one, input_grad, wbuf, d_qkv, lse_t, in_sems, out_sems, gbuf, put_sems,
        ) = refs

        def after(step):
            pass

    def load(sent):
        rows = pl.ds(sent * seq, seq)
        yield pltpu.make_async_copy(qkv_hbm.at[rows, :], qkv.at[rows, :], in_sems.at[2 * sent])
        yield pltpu.make_async_copy(d_mixed_hbm.at[rows, :], d_mixed.at[rows, :], in_sems.at[2 * sent + 1])

    later = [
        pltpu.make_async_copy(src, dst, in_sems.at[2 * (tok // seq) + n])
        for n, (src, dst) in enumerate(((x_hbm, x), (d_one_hbm, d_one), (wq, wbuf)))
    ]
    for sent in range(tok // seq):
        for c in load(sent):
            c.start()
    for c in later:
        c.start()

    lse_t[...] = lse[...].T
    lane = lax.broadcasted_iota(jnp.int32, (seq, 2 * HEAD), 1)
    key = lax.broadcasted_iota(jnp.int32, (seq, 1), 0)

    def stack(m):
        return jnp.concatenate([jnp.where(lane < HEAD, m, 0), jnp.where(lane >= HEAD, m, 0)], axis=0)

    def attend(sent, pair):
        rows = pl.ds(pl.multiple_of(sent * seq, seq), seq)
        q = qkv[rows, cols(pair, 128)] * SCALE
        k = qkv[rows, cols(6 + pair, 128)]
        v = qkv[rows, cols(12 + pair, 128)]
        go = d_mixed[rows, cols(pair, 128)]
        q_two, go_two, k_two = stack(q), stack(go), stack(k * SCALE)
        scores = jnp.where(key < lens[sent], dot_nt(k, q_two), FILL)
        logs = jnp.concatenate([lse_t[pl.ds(2 * pair + h, 1), rows] for h in range(2)], axis=1)
        probs = jnp.exp(scores - logs)
        d_probs = dot_nt(v, go_two)
        delta = jnp.sum(probs * d_probs, axis=0, keepdims=True)
        d_scores = (probs * (d_probs - delta)).astype(bf16)
        d_qkv[rows, cols(12 + pair, 128)] = dot(probs.astype(bf16), go_two).astype(bf16)
        d_qkv[rows, cols(6 + pair, 128)] = dot(d_scores, q_two).astype(bf16)
        turned = jnp.concatenate([d_scores[:, :seq], d_scores[:, seq:]], axis=0)
        d_qkv[rows, cols(pair, 128)] = dot_tn(turned, k_two).astype(bf16)

    def w_grad(g):
        at = [slice(part * D + g * BLK, part * D + (g + 1) * BLK) for part in range(3)]
        got = dot_tn(x[...], jnp.concatenate([d_qkv[:, a] for a in at], axis=1)).astype(bf16)
        for r in range(3):
            for part in range(3):
                block = got[r * BLK:(r + 1) * BLK, part * BLK:(part + 1) * BLK]
                if not comm:
                    gbuf[2 * r:2 * r + 2, :, :, at[part]] = block.reshape(2, TILES, TILE, BLK)
                    continue
                low, high = (
                    block[:, half * LANES:(half + 1) * LANES].reshape(4, 2, 2, TILE, LANES) for half in range(2))
                row = g * GROUP_ROWS + (3 * r + part) * TILE
                mine[:, :, :, REST_ROWS + row:REST_ROWS + row + TILE, :] = jnp.where(p.core == 0, low, high)
                give[:, :, :, row:row + TILE, :] = jnp.where(p.core == 0, high, low)
        if comm:
            sib_copy(3 + g).start()

    after(-1)
    for c in load(0):
        c.wait()
    for c in load(1):
        c.wait()
    for g in range(3):

        def item(n, carry):
            attend(n // 2, 2 * g + n % 2)
            if comm:
                for k in range(4):

                    @pl.when(n == k)
                    def _():
                        after(5 * g + k)
            return carry

        lax.fori_loop(0, 4, item, 0)
        if g == 0:
            later[0].wait()
        w_grad(g)
        after(5 * g + 4)

    for first, third in ((0, 0), (D // LANES, 2)):
        total = col_sum(d_qkv[:, third * D:(third + 1) * D].astype(f32))
        for t in range(D // LANES):
            vec_sum[first + t:first + t + 1, :] = total[:, t * LANES:(t + 1) * LANES]
    if comm:
        vec_sum[2 * D // LANES:, :] = vg_rest[...]
    else:
        puts = [c for n in range(27) for c in put(gbuf, g_qkv, put_sems, n, n // 9, n % 9)]
        for c in puts:
            c.start()
    after(15)

    later[1].wait()
    later[2].wait()
    saves = []
    for sent in range(tok // seq):
        rows = slice(sent * seq, (sent + 1) * seq)
        got = dot_nt(d_qkv[rows, :], wbuf[...].reshape(D, 3 * D)) + d_one[rows, :]
        input_grad[rows, :] = got.astype(bf16)
        saves.append(pltpu.make_async_copy(input_grad.at[rows, :], input_grad_hbm.at[rows, :], out_sems.at[sent]))
        saves[-1].start()
        after(16 + sent)
    for c in saves:
        c.wait()
    if not comm:
        for c in puts:
            c.wait()
        return

    def pick(s, carry):
        block = inverse[s]
        rows = result[jnp.maximum(block, 0)]
        picked[s // per, s % per] = jnp.where(block >= 0, rows, jnp.zeros_like(rows))
        return carry

    lax.fori_loop(0, 16 * per, pick, 0)

    def exchange(k, source):
        there = (p.index + k) % 16
        return remote(picked.at[there], g_own.at[source], xs_send.at[k], xs_recv.at[source], p.at_index(there))

    for k in range(1, 16):
        exchange(k, p.index).start()
    g_own[p.index] = picked[p.index]
    for k in range(1, 16):
        exchange(k, (p.index + k) % 16).wait_recv()
    pair = remote(g_own, g_sib, pair_sems.at[0], pair_sems.at[1], p.sibling)
    pair.start()
    pair.wait_recv()
    for s in range(per):
        here, there = g_own[:, s], g_sib[:, s]
        owned[s, :, :LANES] = jnp.where(p.core == 0, here, there).reshape(BLK, LANES)
        owned[s, :, LANES:] = jnp.where(p.core == 0, there, here).reshape(BLK, LANES)
    pair.wait_send()
    for k in range(1, 16):
        exchange(k, p.index).wait_send()
    for n in range(5):
        vec_copy(n).wait_send()
    for i in range(6):
        sib_copy(i).wait_send()
    sums.end()


def rear(lens, x, qkv, d_mixed, lse, d_one, wq, g_rest=None, vg_rest=None, inverse=None, per=0):
    tok = x.shape[0]
    seq = tok // lens.shape[0]
    hbm = pl.BlockSpec(memory_space=pl.ANY)
    smem, vmem = pl.BlockSpec(memory_space=SMEM), pl.BlockSpec(memory_space=VMEM)
    dma = pltpu.SemaphoreType.DMA
    comm = g_rest is not None
    args = (lens, x, qkv, d_mixed, lse, d_one, wq)
    in_specs = [smem, hbm, hbm, hbm, vmem, hbm, hbm]
    out_shape, out_specs = (jax.ShapeDtypeStruct((tok, D), bf16),), (hbm,)
    scratch = [
        VMEM((tok, D), bf16), VMEM((tok, 3 * D), bf16), VMEM((tok, D), bf16), VMEM((tok, D), f32), VMEM((tok, D), bf16),
        VMEM((6, TILES, TILE, 3 * D), bf16), VMEM((tok, 3 * D), bf16), VMEM((128, tok), f32),
        dma((2 * (tok // seq) + 3,)), dma((tok // seq,)),
    ]
    if comm:
        args += (g_rest.reshape(2, 4, 2, 2, REST_ROWS, LANES), vg_rest, inverse)
        in_specs += [hbm, vmem, smem]
        out_shape += (
            jax.ShapeDtypeStruct((vg_rest.shape[0] + 2 * D // LANES, LANES), f32),
            jax.ShapeDtypeStruct((per, BLK, BLK), bf16),
        )
        out_specs += (vmem, vmem)
        rows = REST_ROWS + QKV_ROWS
        blocks = VMEM((16, per, TILE, LANES), bf16)
        scratch += [
            VMEM((4, 2, 2, rows, LANES), bf16), VMEM((4, 2, 2, rows, LANES), bf16),
            VMEM((8, rows, LANES), bf16), VMEM((4, rows, LANES), bf16), VMEM((4, rows, LANES), bf16),
            VMEM((2, rows, LANES), bf16),
            VMEM((4, 2, 2, QKV_ROWS, LANES), bf16),
            VMEM((ALL, TILE, LANES), bf16),
            blocks, blocks, blocks,
            VMEM((10,) + out_shape[1].shape, f32),
            dma((3,)), dma((6,)), dma((6,)), dma((6, 15)), dma((6, 15)), dma((16,)), dma((16,)), dma((2,)),
            dma((5,)), dma((5,)),
        ]
        params = pltpu.CompilerParams(collective_id=2, has_side_effects=True, vmem_limit_bytes=62 * MIB)
    else:
        out_shape += (
            jax.ShapeDtypeStruct((2 * D // LANES, LANES), f32),
            jax.ShapeDtypeStruct((2, 2, TILES, QKV_ROWS, LANES), bf16),
        )
        out_specs += (vmem, hbm)
        scratch += [VMEM((6, TILES, TILE, 3 * D), bf16), dma((2 * OUT_AT,))]
        params = pltpu.CompilerParams(vmem_limit_bytes=60 * MIB)
    return pl.pallas_call(
        functools.partial(rear_kernel, comm, per, seq),
        out_shape=out_shape,
        in_specs=in_specs,
        out_specs=out_specs,
        scratch_shapes=scratch,
        compiler_params=params,
        name="rear",
    )(*args)


def step_kernel(per, g_hbm, *refs):
    ins, outs, bufs, done = refs[:5], refs[5:9], refs[9:14], refs[14:18]
    g_buf, in_sems, out_sems = refs[18:]

    def loads(s):
        yield pltpu.make_async_copy(g_hbm.at[s], g_buf.at[s], in_sems.at[6 * s])
        for n in range(5):
            yield pltpu.make_async_copy(ins[n].at[s], bufs[n].at[s], in_sems.at[6 * s + 1 + n])

    def stores(s):
        for n in range(4):
            yield pltpu.make_async_copy(done[n].at[s], outs[n].at[s], out_sems.at[4 * s + n])

    for s in range(per):
        for c in loads(s):
            c.start()
    w, ls, rs, lr, rr = bufs
    grad, new_l, new_r, new_w = done
    for first in range(0, per, 2):
        group = range(first, min(first + 2, per))
        for s in group:
            for c in loads(s):
                c.wait()
        for s in group:
            low = g_buf[s]
            grad[s] = low.astype(f32)
            inner = dot(low, rr[s].astype(bf16)).astype(bf16)
            new_l[s] = 0.5 * ls[s] + 0.5 * dot_nt(low, low)
            new_r[s] = 0.5 * rs[s] + 0.5 * dot_tn(low, low)
            new_w[s] = w[s] - dot(lr[s].astype(bf16), inner)
        for s in group:
            for c in stores(s):
                c.start()
    for s in range(per):
        for c in stores(s):
            c.wait()


def owner_step(owned, weights, ls, rs, lr, rr):
    per = weights.shape[0]
    any_spec = pl.BlockSpec(memory_space=pl.ANY)
    dma = pltpu.SemaphoreType.DMA
    return pl.pallas_call(
        functools.partial(step_kernel, per),
        out_shape=(jax.ShapeDtypeStruct(weights.shape, f32),) * 4,
        in_specs=[any_spec] * 6,
        out_specs=(any_spec,) * 4,
        scratch_shapes=[VMEM(weights.shape, f32)] * 9
        + [VMEM(weights.shape, bf16), dma((6 * per,)), dma((4 * per,))],
        compiler_params=pltpu.CompilerParams(vmem_limit_bytes=60 * MIB),
        name="owner_step",
    )(owned, weights, ls, rs, lr, rr)


def from_rows(rows):
    cut = rows.reshape(2, 16, -1, TILE, LANES).transpose(2, 1, 3, 0, 4)
    return cut.reshape(-1, BLK, BLK)


def sum_places():
    def place(b):
        row, part, group = b // 9, (b % 9) // 3, b % 3
        return b - OUT_AT if b >= OUT_AT else ALL - OUT_AT + 9 * group + 3 * row + part

    return [place(b) for b in range(ALL)]


def shards(
    inputs, cotangent, lengths, owner_slot, weights, vectors,
    left_stat, right_stat, left_root, right_root, vector_stat,
):
    per, size = weights.shape[0], vectors.shape[0]
    chips = lax.axis_size("fsdp")
    chip, core = lax.axis_index("fsdp"), lax.axis_index("dp")
    comm = chips == 16
    slots = jnp.arange(chips * per, dtype=jnp.int32)
    tail = jnp.pad(vectors.astype(bf16), (0, TAIL * LANES - size)).reshape(TAIL, LANES)
    if comm:
        role = slots // per
        turned = (role // 4) * 4 + (role % 2) * 2 + (role // 2) % 2
        by_role = jnp.where(core == 0, slots, turned * per + slots % per)
        numbers = jnp.asarray(sum_places(), jnp.int32) + 1
        inverse = jnp.sum(jnp.where(by_role[:, None] == owner_slot[None, :], numbers[None, :], 0), axis=1) - 1
        w_all, tails = gather(weights, tail)
    else:
        low = weights.astype(bf16).reshape(per, 2, HALF, BLK).transpose(1, 0, 2, 3)
        w_all = lax.all_gather(low, "fsdp", axis=1, tiled=True)
        tails = lax.all_gather(tail, "fsdp", axis=0)
    vec = tails.reshape(chips, TAIL * LANES)[:, :size].reshape(1, -1).astype(f32)
    w_all = w_all.reshape(2, -1, TILE, BLK)
    qkv, mixed, lse, wq = front(owner_slot, lengths, inputs, w_all, vec)
    outputs, d_one, d_mixed, vg_rest, g_rest = middle(
        owner_slot, lengths, inputs, cotangent, mixed, vec, w_all)
    if comm:
        input_grad, vec_sum, owned = rear(
            lengths, inputs, qkv, d_mixed, lse, d_one, wq, g_rest, vg_rest, inverse, per)
    else:
        input_grad, vg_qv, g_qkv = rear(lengths, inputs, qkv, d_mixed, lse, d_one, wq)
        vec_sum = lax.psum(jnp.concatenate([vg_qv, vg_rest], axis=0), ("dp", "fsdp"))
        blocks = from_rows(jnp.concatenate([g_qkv, g_rest], axis=3)).astype(f32)
        by_slot = jnp.zeros((chips * per, BLK, BLK), f32).at[owner_slot].set(blocks)
        owned = lax.psum(lax.psum_scatter(by_slot, "fsdp", scatter_dimension=0, tiled=True), "dp").astype(bf16)
    grad, new_left, new_right, new_weights = owner_step(
        owned, weights, left_stat, right_stat, left_root, right_root)
    vec_grad = lax.dynamic_slice(vec_sum.reshape(-1), (chip * size,), (size,))
    new_stat = 0.5 * vector_stat + 0.5 * vec_grad * vec_grad
    new_vectors = vectors - 0.1 * vec_grad * lax.rsqrt(new_stat + VEC_EPS)
    return (outputs, input_grad, grad, new_left, new_right, new_weights, vec_grad, new_stat, new_vectors)


def solution(mesh):
    tokens = P(("dp", "fsdp"), None)
    blocks, packed = P("fsdp", None, None), P("fsdp")
    return jax.shard_map(
        shards,
        mesh=mesh,
        in_specs=(tokens, tokens, P(("dp", "fsdp")), P(), blocks, packed, blocks, blocks, blocks, blocks, packed),
        out_specs=(tokens, tokens, blocks, blocks, blocks, blocks, packed, packed, packed),
        check_vma=False,
    )
```
